512 devices in a mesh: ew: 32 (over z, x_hi), ns: 16 (over y, x_lo, core).
Axes of the slice: x: 4 (x_hi: 2, x_lo: 2; x = x_hi * 2 + x_lo), y: 4, z: 16, core: 2. Of those that a mesh axis runs over, the one named last changes fastest.
Arguments:
- frame: bfloat16 [8, 256, 4096], P(None, 'ns', 'ew'), may hold values from -6 to 6
- hidden_prev: bfloat16 [64, 256, 4096], P(None, 'ns', 'ew'), may hold values from -0.94921875 to 0.94921875
- cell_prev: float32 [64, 256, 4096], P(None, 'ns', 'ew'), may hold values from -6 to 6
- kernel: bfloat16 [256, 648], replicated, may hold values from -0.25 to 0.25
- bias: float32 [256], replicated, may hold values from -4 to 4
- grad_hidden: float32 [64, 256, 4096], P(None, 'ns', 'ew'), may hold values from -6 to 6
- grad_cell: float32 [64, 256, 4096], P(None, 'ns', 'ew'), may hold values from -6 to 6
Outputs:
- hidden: bfloat16 [64, 256, 4096], P(None, 'ns', 'ew')
- cell: float32 [64, 256, 4096], P(None, 'ns', 'ew')
- grad_frame: bfloat16 [8, 256, 4096], P(None, 'ns', 'ew')
- grad_hidden_prev: bfloat16 [64, 256, 4096], P(None, 'ns', 'ew')
- grad_cell_prev: float32 [64, 256, 4096], P(None, 'ns', 'ew')
- kernel_step: float32 [256, 648], replicated
- bias_step: float32 [256], replicated
The draws below stay inside these ranges and needn't reach their ends.
All inputs are finite; a program needn't handle non-finite values.
Results may differ from the reference program's by a relative error of at most 0.0049.
Values may be sent and summed in bfloat16 or wider, within the bound.
No kernel may reach another device: no remote copies, remote signals or barrier semaphores. Data moves between devices by JAX's collectives and lax.ppermute only.
A program may use at most 128 MiB of HBM per device.

```python
import jax
import jax.numpy as jnp
from jax import lax

CIN = 8
HID = 64
CT = 72
GATES = 256
NN = 256
NE = 4096


def block_levels(own_key, shape, split, low, top_value):
    def one(dim, shards_of):
        draws = jax.random.uniform(jax.random.fold_in(jax.random.fold_in(own_key, 6), dim), (shards_of,), jnp.float32, low / len(split), top_value / len(split))
        return jnp.repeat(jnp.exp(draws), shape[dim] // shards_of).reshape((-1,) + (1,) * (len(shape) - dim - 1))

    loudness = one(*split[0])
    for cut in split[1:]:
        loudness = loudness * one(*cut)
    return loudness


def gaussian(own_key, shape, spread, most, shards=(), kind=jnp.bfloat16):
    drawn = spread * jax.random.normal(own_key, shape, jnp.float32)
    if shards:
        drawn = drawn * block_levels(own_key, shape, shards, -0.22, 0.18)
    return jnp.clip(drawn, -most, most).astype(kind)


def setup_inputs(seed: int = 0) -> dict:
    arg_keys = jax.random.split(jax.random.key(seed), 8)
    frame = gaussian(arg_keys[0], (CIN, NN, NE), 1.0, 6.0, ((1, 16), (2, 32)))
    hidden_prev = jnp.clip(jax.random.uniform(arg_keys[1], (HID, NN, NE), jnp.float32, -0.94921875, 0.94921875) * block_levels(arg_keys[1], (HID, NN, NE), ((1, 16), (2, 32)), -0.4, 0.0), -0.94921875, 0.94921875).astype(jnp.bfloat16)
    cell_prev = gaussian(arg_keys[2], (HID, NN, NE), 1.0, 6.0, ((1, 16), (2, 32)), jnp.float32)
    kernel = gaussian(arg_keys[3], (GATES, 9 * CT), (9 * CT) ** -0.5, 0.25)
    bias = gaussian(arg_keys[4], (GATES,), 1.0, 4.0, (), jnp.float32)
    grad_hidden = gaussian(arg_keys[5], (HID, NN, NE), 1.0, 6.0, ((1, 16), (2, 32)), jnp.float32)
    grad_cell = gaussian(arg_keys[6], (HID, NN, NE), 1.0, 6.0, ((1, 16), (2, 32)), jnp.float32)
    return {"frame": frame, "hidden_prev": hidden_prev, "cell_prev": cell_prev, "kernel": kernel, "bias": bias, "grad_hidden": grad_hidden, "grad_cell": grad_cell}


CLIP_NORM = 100.0

def cell_step(gate_sums, cell_prev, grad_hidden, grad_cell):
    units = cell_prev.shape[0]
    input_gate = jax.nn.sigmoid(gate_sums[:units])
    forget_gate = jax.nn.sigmoid(gate_sums[units:2 * units])
    cand_gate = jnp.tanh(gate_sums[2 * units:3 * units])
    output_gate = jax.nn.sigmoid(gate_sums[3 * units:])
    cell = forget_gate * cell_prev + input_gate * cand_gate
    cell_tanh = jnp.tanh(cell)
    hidden = (output_gate * cell_tanh).astype(jnp.bfloat16)
    cell_grad = grad_cell + grad_hidden * output_gate * (1.0 - cell_tanh * cell_tanh)
    grad_gates = jnp.concatenate([cell_grad * cand_gate * input_gate * (1.0 - input_gate), cell_grad * cell_prev * forget_gate * (1.0 - forget_gate), cell_grad * input_gate * (1.0 - cand_gate * cand_gate), grad_hidden * cell_tanh * output_gate * (1.0 - output_gate)], 0).astype(jnp.bfloat16)
    return (hidden, cell, grad_gates, cell_grad * forget_gate)

def reference(frame, hidden_prev, cell_prev, kernel, bias, grad_hidden, grad_cell):
    joined = jnp.concatenate([frame, hidden_prev], 0)
    channels, height, breadth = joined.shape
    gate_rows = kernel.shape[0]
    padded = jnp.pad(joined, ((0, 0), (1, 1), (1, 1)))
    gate_sums = jnp.zeros((gate_rows, height * breadth), jnp.float32)
    for row_off in range(3):
        for col_off in range(3):
            offset = 3 * row_off + col_off
            window = padded[:, row_off:row_off + height, col_off:col_off + breadth].reshape(channels, -1)
            gate_sums = gate_sums + jnp.dot(kernel[:, offset * channels:(offset + 1) * channels], window, preferred_element_type=jnp.float32)
    gate_sums = (gate_sums + bias[:, None]).reshape(gate_rows, height, breadth)
    hidden, cell, grad_gates, grad_cell_prev = cell_step(gate_sums, cell_prev, grad_hidden, grad_cell)
    flat_grads = grad_gates.reshape(gate_rows, -1)
    padded_grads = jnp.pad(grad_gates, ((0, 0), (1, 1), (1, 1)))
    blocks = []
    joined_grad = jnp.zeros((channels, height * breadth), jnp.float32)
    for row_off in range(3):
        for col_off in range(3):
            offset = 3 * row_off + col_off
            window = padded[:, row_off:row_off + height, col_off:col_off + breadth].reshape(channels, -1)
            blocks.append(lax.dot_general(flat_grads, window, (((1,), (1,)), ((), ())), preferred_element_type=jnp.float32))
            moved = padded_grads[:, 2 - row_off:2 - row_off + height, 2 - col_off:2 - col_off + breadth].reshape(gate_rows, -1)
            joined_grad = joined_grad + lax.dot_general(kernel[:, offset * channels:(offset + 1) * channels], moved, (((0,), (0,)), ((), ())), preferred_element_type=jnp.float32)
    weight_grad = jnp.concatenate(blocks, 1)
    bias_grad = lax.optimization_barrier(jnp.sum(grad_gates.astype(jnp.float32), axis=(1, 2)))
    joined_grad = joined_grad.reshape(channels, height, breadth)
    inputs_count = frame.shape[0]
    grad_frame = joined_grad[:inputs_count].astype(jnp.bfloat16)
    grad_hidden_prev = joined_grad[inputs_count:].astype(jnp.bfloat16)
    grad_norm = jnp.sqrt(jnp.sum(weight_grad * weight_grad) + jnp.sum(bias_grad * bias_grad))
    factor = jnp.minimum(1.0, CLIP_NORM / grad_norm)
    return (hidden, cell, grad_frame, grad_hidden_prev, grad_cell_prev, weight_grad * factor, bias_grad * factor)
```

```python
import jax
import jax.numpy as jnp
from jax import lax
from jax.sharding import Mesh, PartitionSpec as P

CLIP_NORM = 100.0
EW = ("z", "x_hi")
NS = ("y", "x_lo", "core")
PLANE = ("x_hi", "y", "x_lo", "core")


def padded_2(block, sides, width):
    for axis, dim in sides:
        count = lax.axis_size(axis)
        forward = [(i, i + 1) for i in range(count - 1)]
        backward = [(target, source) for source, target in forward]
        low = lax.ppermute(
            lax.slice_in_dim(block, block.shape[dim] - width, None, axis=dim), axis, forward
        )
        high = lax.ppermute(lax.slice_in_dim(block, 0, width, axis=dim), axis, backward)
        block = jnp.concatenate([low, block, high], axis=dim)
    return block


def cell_step(gate_sums, cell_prev, grad_hidden, grad_cell):
    units = cell_prev.shape[0]
    input_gate = jax.nn.sigmoid(gate_sums[:units])
    forget_gate = jax.nn.sigmoid(gate_sums[units : 2 * units])
    cand_gate = jnp.tanh(gate_sums[2 * units : 3 * units])
    output_gate = jax.nn.sigmoid(gate_sums[3 * units :])
    cell = forget_gate * cell_prev + input_gate * cand_gate
    cell_tanh = jnp.tanh(cell)
    hidden = (output_gate * cell_tanh).astype(jnp.bfloat16)
    cell_grad = grad_cell + grad_hidden * output_gate * (1.0 - cell_tanh * cell_tanh)
    grad_gates = jnp.concatenate(
        [
            cell_grad * cand_gate * input_gate * (1.0 - input_gate),
            cell_grad * cell_prev * forget_gate * (1.0 - forget_gate),
            cell_grad * input_gate * (1.0 - cand_gate * cand_gate),
            grad_hidden * cell_tanh * output_gate * (1.0 - output_gate),
        ],
        0,
    ).astype(jnp.bfloat16)
    return (hidden, cell, grad_gates, cell_grad * forget_gate)


def build_patches(padded, height, breadth):
    channels = padded.shape[0]
    windows = [
        padded[:, row_off : row_off + height, col_off : col_off + breadth]
        for row_off in range(3)
        for col_off in range(3)
    ]
    return jnp.stack(windows, 0).reshape(9 * channels, height * breadth)


def spread_back(kernel, padded_grads, height, breadth):
    gate_rows = kernel.shape[0]
    channels = kernel.shape[1] // 9
    product = lax.dot_general(
        kernel,
        padded_grads.reshape(gate_rows, -1),
        (((0,), (0,)), ((), ())),
        preferred_element_type=jnp.float32,
    )
    product = product.reshape(9, channels, height + 2, breadth + 2)
    total = jnp.zeros((channels, height, breadth), jnp.float32)
    for row_off in range(3):
        for col_off in range(3):
            total = (
                total
                + product[
                    3 * row_off + col_off,
                    :,
                    2 - row_off : 2 - row_off + height,
                    2 - col_off : 2 - col_off + breadth,
                ]
            )
    return total


def sum_everywhere(weight_local, bias_local):
    rows, columns = weight_local.shape
    width = -(-(columns + 1) // 128) * 128
    terms = jnp.concatenate([weight_local, bias_local[:, None]], 1)
    terms = jnp.pad(terms, ((0, 0), (0, width - columns - 1))).astype(jnp.bfloat16)
    plane = lax.axis_size(PLANE)
    deep = lax.axis_size("z")
    share = rows // plane
    mine = lax.all_to_all(terms, PLANE, 0, 0, tiled=True).reshape(plane, share, width)
    mine = jnp.sum(mine.astype(jnp.float32), 0)
    mine = jnp.broadcast_to(mine[None], (deep, share, width))
    mine = lax.all_to_all(mine, "z", 0, 0, tiled=True)
    mine = jnp.sum(mine, 0).astype(jnp.bfloat16)
    mine = jnp.broadcast_to(mine[None], (plane, share, width)).reshape(rows, width)
    total = lax.all_to_all(mine, PLANE, 0, 0, tiled=True).astype(jnp.float32)
    return total[:, :columns], total[:, columns]


def per_device(frame, hidden_prev, cell_prev, kernel, bias, grad_hidden, grad_cell):
    joined = jnp.concatenate([frame, hidden_prev], 0)
    channels, height, breadth = joined.shape
    gate_rows = kernel.shape[0]
    padded = padded_2(joined, ((EW, 2), (NS, 1)), 1)
    inner = build_patches(padded, height, breadth)
    gate_sums = jnp.dot(kernel, inner, preferred_element_type=jnp.float32) + bias[:, None]
    gate_sums = gate_sums.reshape(gate_rows, height, breadth)
    hidden, cell, grad_gates, grad_cell_prev = cell_step(
        gate_sums, cell_prev, grad_hidden, grad_cell
    )
    padded_grads = padded_2(grad_gates, ((EW, 2), (NS, 1)), 1)
    weight_local = lax.dot_general(
        grad_gates.reshape(gate_rows, -1),
        inner,
        (((1,), (1,)), ((), ())),
        preferred_element_type=jnp.float32,
    )
    bias_local = jnp.sum(grad_gates.astype(jnp.float32), axis=(1, 2))
    joined_grad = spread_back(kernel, padded_grads, height, breadth)
    inputs_count = frame.shape[0]
    grad_frame = joined_grad[:inputs_count].astype(jnp.bfloat16)
    grad_hidden_prev = joined_grad[inputs_count:].astype(jnp.bfloat16)
    weight_grad, bias_grad = sum_everywhere(weight_local, bias_local)
    total_norm = jnp.sqrt(jnp.sum(weight_grad * weight_grad) + jnp.sum(bias_grad * bias_grad))
    factor = jnp.minimum(1.0, CLIP_NORM / total_norm)
    kernel_step = weight_grad * factor
    return (
        hidden,
        cell,
        grad_frame,
        grad_hidden_prev,
        grad_cell_prev,
        kernel_step,
        bias_grad * factor,
    )


def solution(mesh):
    mesh = Mesh(mesh.devices.reshape(16, 2, 4, 2, 2), EW + NS)
    placed = (
        P(None, NS, EW),
        P(None, NS, EW),
        P(None, NS, EW),
        P(),
        P(),
        P(None, NS, EW),
        P(None, NS, EW),
    )
    return jax.shard_map(
        per_device,
        mesh=mesh,
        in_specs=placed,
        out_specs=(
            P(None, NS, EW),
            P(None, NS, EW),
            P(None, NS, EW),
            P(None, NS, EW),
            P(None, NS, EW),
            P(),
            P(),
        ),
        check_vma=False,
    )
```

```python
import jax
import jax.numpy as jnp
from jax import lax
from jax.experimental import pallas as pl
from jax.experimental.pallas import tpu as pltpu
from jax.sharding import Mesh, PartitionSpec as P

CLIP_NORM = 100.0
EW = ("z", "x_hi")
NS = ("y", "x_lo", "core")
PLANE = ("x_hi", "y", "x_lo", "core")
LANES = 128
STACK = 256
BF16 = jnp.bfloat16
F32 = jnp.float32


def vmem(count):
    return [pl.BlockSpec(memory_space=pltpu.VMEM)] * count


def neighbours(low_side, high_side, axes):
    count = lax.axis_size(axes)
    forward = [(i, i + 1) for i in range(count - 1)]
    backward = [(target, source) for source, target in forward]
    return lax.ppermute(high_side, axes, forward), lax.ppermute(low_side, axes, backward)


def sigmoid(x):
    return 0.5 * jnp.tanh(0.5 * x) + 0.5


def forward_kernel(
    frame, hidden_prev, top, bottom, left, right, weights, bias, cell_prev, grad_hidden, grad_cell,
    hidden, cell, grad_cell_prev, grads, edges, terms,
    joined, stacked, hidden_rows,
):
    height = grads.shape[1] // LANES
    units = hidden_prev.shape[0] // height
    inputs = frame.shape[0] // height
    channels = inputs + units
    joined[: inputs * height] = frame[...].astype(F32)
    joined[inputs * height :] = hidden_prev[...].astype(F32)
    lane = lax.broadcasted_iota(jnp.int32, (channels, LANES), 1)
    left_cells = left[...].astype(F32)
    right_cells = right[...].astype(F32)
    spare = STACK - 3 * channels
    ones_row = (lax.broadcasted_iota(jnp.int32, (spare, LANES), 0) == 0).astype(F32)
    for place in range(height + 2):
        if place == 0:
            row = top[...].astype(F32)
        elif place == height + 1:
            row = bottom[...].astype(F32)
        else:
            row = joined[pl.ds(place - 1, channels, stride=height), :]
        before = jnp.where(lane == 0, pltpu.roll(left_cells, (LANES - place) % LANES, 1), pltpu.roll(row, 1, 1))
        after = jnp.where(
            lane == LANES - 1, pltpu.roll(right_cells, LANES - 1 - place, 1), pltpu.roll(row, LANES - 1, 1)
        )
        stacked[:, place * LANES : (place + 1) * LANES] = jnp.concatenate([before, row, after, ones_row], 0).astype(
            BF16
        )
    bias_cells = jnp.broadcast_to(bias[...], (4 * units, LANES))
    for pair in range(height // 2):
        sums = jnp.zeros((4 * units, 2 * LANES), F32)
        for row_off in range(3):
            start = (2 * pair + row_off) * LANES
            sums = sums + jnp.dot(
                weights[:, row_off * STACK : (row_off + 1) * STACK],
                stacked[:, start : start + 2 * LANES],
                preferred_element_type=F32,
            )
        for half in range(2):
            n = 2 * pair + half
            at = pl.ds(n, units, stride=height)
            gates = sums[:, half * LANES : (half + 1) * LANES] + bias_cells
            input_gate = sigmoid(gates[:units])
            forget_gate = sigmoid(gates[units : 2 * units])
            cand_gate = jnp.tanh(gates[2 * units : 3 * units])
            output_gate = sigmoid(gates[3 * units :])
            old = cell_prev[at, :]
            down = grad_hidden[at, :]
            new = forget_gate * old + input_gate * cand_gate
            new_tanh = jnp.tanh(new)
            cell[at, :] = new
            hidden_rows[at, :] = output_gate * new_tanh
            cell_grad = grad_cell[at, :] + down * output_gate * (1.0 - new_tanh * new_tanh)
            grad_cell_prev[at, :] = cell_grad * forget_gate
            grads[:, n * LANES : (n + 1) * LANES] = jnp.concatenate(
                [
                    cell_grad * cand_gate * input_gate * (1.0 - input_gate),
                    cell_grad * old * forget_gate * (1.0 - forget_gate),
                    cell_grad * input_gate * (1.0 - cand_gate * cand_gate),
                    down * new_tanh * output_gate * (1.0 - output_gate),
                ],
                0,
            ).astype(BF16)
    hidden[...] = hidden_rows[...].astype(BF16)
    for row_off in range(3):
        terms[row_off * STACK : (row_off + 1) * STACK] = lax.dot_general(
            stacked[:, row_off * LANES : (row_off + height) * LANES],
            grads[...],
            (((1,), (1,)), ((), ())),
            preferred_element_type=F32,
        ).astype(BF16)
    source = lax.broadcasted_iota(jnp.int32, (height * LANES, LANES), 0)
    target = lax.broadcasted_iota(jnp.int32, (height * LANES, LANES), 1)
    wanted = jnp.where(target < height, target * LANES, (target - height) * LANES + LANES - 1)
    pick = ((source == wanted) & (target < 2 * height)).astype(F32).astype(BF16)
    edges[...] = jnp.dot(grads[...], pick, preferred_element_type=F32).astype(BF16)


def backward_kernel(weights, grads, top, bottom, left, right, grad_frame, grad_hidden_prev, sums, rows):
    height = grads.shape[1] // LANES
    inputs = grad_frame.shape[0] // height
    channels = rows.shape[0] // height
    lane = lax.broadcasted_iota(jnp.int32, (channels, LANES), 1)
    outer = jnp.dot(weights[...], jnp.concatenate([left[...], right[...]], 1), preferred_element_type=F32)
    first = jnp.zeros((channels, LANES), F32)
    last = jnp.zeros((channels, LANES), F32)
    for row_off in range(3):
        low, high = 3 * row_off * channels, (3 * row_off + 2) * channels
        first = first + pltpu.roll(outer[high : high + channels, :LANES], (LANES - 2 + row_off) % LANES, 1)
        last = last + pltpu.roll(outer[low : low + channels, LANES:], (LANES - 2 + row_off) % LANES, 1)
    for place in range(0, height + 2, 2):
        if place == 0:
            cells = jnp.concatenate([top[...], grads[:, :LANES]], 1)
        elif place == height:
            cells = jnp.concatenate([grads[:, (height - 1) * LANES :], bottom[...]], 1)
        else:
            cells = grads[:, (place - 1) * LANES : (place + 1) * LANES]
        product = jnp.dot(weights[...], cells, preferred_element_type=F32)
        for half in range(2):
            for row_off in range(3):
                n = place + half - 1 + row_off - 1
                if not 0 <= n < height:
                    continue
                for col_off in range(3):
                    start = (3 * row_off + col_off) * channels
                    piece = product[start : start + channels, half * LANES : (half + 1) * LANES]
                    if row_off == 2 or (place + half == 0):
                        sums[n, col_off] = piece
                    else:
                        sums[n, col_off] = sums[n, col_off] + piece
    for n in range(height):
        total = sums[n, 1]
        total = total + jnp.where(
            lane == LANES - 1, pltpu.roll(last, LANES - 1 - n, 1), pltpu.roll(sums[n, 0], LANES - 1, 1)
        )
        total = total + jnp.where(
            lane == 0, pltpu.roll(first, (LANES - n) % LANES, 1), pltpu.roll(sums[n, 2], 1, 1)
        )
        rows[pl.ds(n, channels, stride=height), :] = total
    grad_frame[...] = rows[: inputs * height].astype(BF16)
    grad_hidden_prev[...] = rows[inputs * height :].astype(BF16)


def finish_kernel(total, kernel_step, bias_step):
    block = kernel_step.shape[0] // 3
    parts = [total[i * STACK : i * STACK + block].astype(F32) for i in range(3)]
    bias_grad = total[block : block + 8].astype(F32)[:1]
    norm = jnp.sqrt(sum(jnp.sum(part * part) for part in parts) + jnp.sum(bias_grad * bias_grad))
    factor = jnp.minimum(1.0, CLIP_NORM / norm)
    for i, part in enumerate(parts):
        kernel_step[i * block : (i + 1) * block] = part * factor
    bias_step[...] = bias_grad * factor


def sum_everywhere(terms):
    rows, width = terms.shape
    plane = lax.axis_size(PLANE)
    deep = lax.axis_size("z")
    share = rows // plane
    mine = lax.all_to_all(terms, PLANE, 0, 0, tiled=True).reshape(plane, share, width)
    mine = jnp.sum(mine.astype(F32), 0)
    mine = jnp.broadcast_to(mine[None], (deep, share, width))
    mine = lax.all_to_all(mine, "z", 0, 0, tiled=True)
    mine = jnp.sum(mine, 0).astype(BF16)
    mine = jnp.broadcast_to(mine[None], (plane, share, width)).reshape(rows, width)
    return lax.all_to_all(mine, PLANE, 0, 0, tiled=True)


def end_columns(top, low, high, bottom):
    spare = ((0, 0), (0, LANES - low.shape[1] - 2))
    return (
        jnp.pad(jnp.concatenate([top[:, :1], low, bottom[:, :1]], 1), spare),
        jnp.pad(jnp.concatenate([top[:, -1:], high, bottom[:, -1:]], 1), spare),
    )


def shape(rows, columns, kind):
    return jax.ShapeDtypeStruct((rows, columns), kind)


def per_device(frame, hidden_prev, cell_prev, kernel, bias, grad_hidden, grad_cell):
    inputs, height, breadth = frame.shape
    units = hidden_prev.shape[0]
    channels = inputs + units
    gate_rows = kernel.shape[0]
    cells = height * breadth
    row = jnp.concatenate([frame[:, 0], hidden_prev[:, 0]], 0)
    last_row = jnp.concatenate([frame[:, -1], hidden_prev[:, -1]], 0)
    column = jnp.concatenate([frame[:, :, 0], hidden_prev[:, :, 0]], 0)
    last_column = jnp.concatenate([frame[:, :, -1], hidden_prev[:, :, -1]], 0)
    weights = kernel.reshape(gate_rows, 3, 3 * channels)
    weights = jnp.pad(weights, ((0, 0), (0, 0), (0, STACK - 3 * channels))).reshape(gate_rows, 3 * STACK)
    weights_back = kernel.T
    top, bottom = neighbours(row, last_row, NS)
    left, right = neighbours(*end_columns(top, column, last_column, bottom), EW)

    hidden, cell, grad_cell_prev, grads, edges, terms = pl.pallas_call(
        forward_kernel,
        out_shape=(
            shape(units * height, breadth, BF16),
            shape(units * height, breadth, F32),
            shape(units * height, breadth, F32),
            shape(gate_rows, cells, BF16),
            shape(gate_rows, LANES, BF16),
            shape(3 * STACK, gate_rows, BF16),
        ),
        in_specs=vmem(11),
        out_specs=tuple(vmem(6)),
        scratch_shapes=[
            pltpu.VMEM((channels * height, breadth), F32),
            pltpu.VMEM((STACK, (height + 2) * breadth), BF16),
            pltpu.VMEM((units * height, breadth), F32),
        ],
        compiler_params=pltpu.CompilerParams(vmem_limit_bytes=40 * 2**20),
        cost_estimate=pl.CostEstimate(flops=1_400_000_000, bytes_accessed=6_000_000, transcendentals=700_000),
    )(
        frame.reshape(inputs * height, breadth),
        hidden_prev.reshape(units * height, breadth),
        top,
        bottom,
        left,
        right,
        weights,
        bias[:, None],
        cell_prev.reshape(units * height, breadth),
        grad_hidden.reshape(units * height, breadth),
        grad_cell.reshape(units * height, breadth),
    )

    grad_top, grad_bottom = neighbours(grads[:, :LANES], grads[:, cells - LANES :], NS)
    grad_left, grad_right = neighbours(
        *end_columns(grad_top, edges[:, :height], edges[:, height : 2 * height], grad_bottom), EW
    )
    total = sum_everywhere(terms)
    grad_frame, grad_hidden_prev = pl.pallas_call(
        backward_kernel,
        out_shape=(shape(inputs * height, breadth, BF16), shape(units * height, breadth, BF16)),
        in_specs=vmem(6),
        out_specs=tuple(vmem(2)),
        scratch_shapes=[
            pltpu.VMEM((height, 3, channels, breadth), F32),
            pltpu.VMEM((channels * height, breadth), F32),
        ],
        compiler_params=pltpu.CompilerParams(vmem_limit_bytes=40 * 2**20),
        cost_estimate=pl.CostEstimate(flops=764_000_000, bytes_accessed=3_000_000, transcendentals=0),
    )(weights_back, grads, grad_top, grad_bottom, grad_left, grad_right)
    kernel_step, bias_step = pl.pallas_call(
        finish_kernel,
        out_shape=(shape(9 * channels, gate_rows, F32), shape(1, gate_rows, F32)),
        in_specs=vmem(1),
        out_specs=tuple(vmem(2)),
        compiler_params=pltpu.CompilerParams(vmem_limit_bytes=40 * 2**20),
    )(total)
    whole = (units, height, breadth)
    return (
        hidden.reshape(whole),
        cell.reshape(whole),
        grad_frame.reshape(frame.shape),
        grad_hidden_prev.reshape(whole),
        grad_cell_prev.reshape(whole),
        kernel_step.T,
        bias_step.reshape(gate_rows),
    )


def solution(mesh):
    mesh = Mesh(mesh.devices.reshape(16, 2, 4, 2, 2), EW + NS)
    grid = P(None, NS, EW)
    return jax.shard_map(
        per_device,
        mesh=mesh,
        in_specs=(grid, grid, grid, P(), P(), grid, grid),
        out_specs=(grid, grid, grid, grid, grid, P(), P()),
        check_vma=False,
    )
```

```python
import jax
import jax.numpy as jnp
from jax import lax
from jax.experimental import pallas as pl
from jax.experimental.pallas import tpu as pltpu
from jax.sharding import Mesh, PartitionSpec as P

CLIP_NORM = 100.0
EW = ("z_hi", "z_lo", "x_hi")
NS = ("y", "x_lo", "core")
PLANE = ("x_hi", "y", "x_lo", "core")
LANES = 128
STACK = 256
BF16 = jnp.bfloat16
F32 = jnp.float32


def vmem(count):
    return [pl.BlockSpec(memory_space=pltpu.VMEM)] * count


def neighbours(low_side, high_side, axes):
    count = lax.axis_size(axes)
    forward = [(i, i + 1) for i in range(count - 1)]
    backward = [(target, source) for source, target in forward]
    return lax.ppermute(high_side, axes, forward), lax.ppermute(low_side, axes, backward)


def sigmoid(x):
    return 0.5 * jnp.tanh(0.5 * x) + 0.5


def forward_kernel(
    frame, hidden_prev, top, bottom, left, right, weights, bias, cell_prev, grad_hidden, grad_cell,
    hidden, cell, grad_cell_prev, grads, edges, terms,
    joined, stacked, hidden_rows,
):
    height = grads.shape[1] // LANES
    units = hidden_prev.shape[0] // height
    inputs = frame.shape[0] // height
    channels = inputs + units
    joined[: inputs * height] = frame[...].astype(F32)
    joined[inputs * height :] = hidden_prev[...].astype(F32)
    lane = lax.broadcasted_iota(jnp.int32, (channels, LANES), 1)
    left_cells = left[...].astype(F32)
    right_cells = right[...].astype(F32)
    spare = STACK - 3 * channels
    ones_row = (lax.broadcasted_iota(jnp.int32, (spare, LANES), 0) == 0).astype(F32)
    for place in range(height + 2):
        if place == 0:
            row = top[...].astype(F32)
        elif place == height + 1:
            row = bottom[...].astype(F32)
        else:
            row = joined[pl.ds(place - 1, channels, stride=height), :]
        before = jnp.where(lane == 0, pltpu.roll(left_cells, (LANES - place) % LANES, 1), pltpu.roll(row, 1, 1))
        after = jnp.where(
            lane == LANES - 1, pltpu.roll(right_cells, LANES - 1 - place, 1), pltpu.roll(row, LANES - 1, 1)
        )
        stacked[:, place * LANES : (place + 1) * LANES] = jnp.concatenate([before, row, after, ones_row], 0).astype(
            BF16
        )
    bias_cells = jnp.broadcast_to(bias[...], (4 * units, LANES))
    for pair in range(height // 2):
        sums = jnp.zeros((4 * units, 2 * LANES), F32)
        for row_off in range(3):
            start = (2 * pair + row_off) * LANES
            sums = sums + jnp.dot(
                weights[:, row_off * STACK : (row_off + 1) * STACK],
                stacked[:, start : start + 2 * LANES],
                preferred_element_type=F32,
            )
        for half in range(2):
            n = 2 * pair + half
            at = pl.ds(n, units, stride=height)
            gates = sums[:, half * LANES : (half + 1) * LANES] + bias_cells
            input_gate = sigmoid(gates[:units])
            forget_gate = sigmoid(gates[units : 2 * units])
            cand_gate = jnp.tanh(gates[2 * units : 3 * units])
            output_gate = sigmoid(gates[3 * units :])
            old = cell_prev[at, :]
            down = grad_hidden[at, :]
            new = forget_gate * old + input_gate * cand_gate
            new_tanh = jnp.tanh(new)
            cell[at, :] = new
            hidden_rows[at, :] = output_gate * new_tanh
            cell_grad = grad_cell[at, :] + down * output_gate * (1.0 - new_tanh * new_tanh)
            grad_cell_prev[at, :] = cell_grad * forget_gate
            grads[:, n * LANES : (n + 1) * LANES] = jnp.concatenate(
                [
                    cell_grad * cand_gate * input_gate * (1.0 - input_gate),
                    cell_grad * old * forget_gate * (1.0 - forget_gate),
                    cell_grad * input_gate * (1.0 - cand_gate * cand_gate),
                    down * new_tanh * output_gate * (1.0 - output_gate),
                ],
                0,
            ).astype(BF16)
    hidden[...] = hidden_rows[...].astype(BF16)
    for row_off in range(3):
        terms[row_off * STACK : (row_off + 1) * STACK] = lax.dot_general(
            stacked[:, row_off * LANES : (row_off + height) * LANES],
            grads[...],
            (((1,), (1,)), ((), ())),
            preferred_element_type=F32,
        ).astype(BF16)
    source = lax.broadcasted_iota(jnp.int32, (height * LANES, LANES), 0)
    target = lax.broadcasted_iota(jnp.int32, (height * LANES, LANES), 1)
    wanted = jnp.where(target < height, target * LANES, (target - height) * LANES + LANES - 1)
    pick = ((source == wanted) & (target < 2 * height)).astype(F32).astype(BF16)
    edges[...] = jnp.dot(grads[...], pick, preferred_element_type=F32).astype(BF16)


def backward_kernel(weights, grads, top, bottom, left, right, grad_frame, grad_hidden_prev, sums, rows):
    height = grads.shape[1] // LANES
    inputs = grad_frame.shape[0] // height
    channels = rows.shape[0] // height
    lane = lax.broadcasted_iota(jnp.int32, (channels, LANES), 1)
    outer = jnp.dot(weights[...], jnp.concatenate([left[...], right[...]], 1), preferred_element_type=F32)
    first = jnp.zeros((channels, LANES), F32)
    last = jnp.zeros((channels, LANES), F32)
    for row_off in range(3):
        low, high = 3 * row_off * channels, (3 * row_off + 2) * channels
        first = first + pltpu.roll(outer[high : high + channels, :LANES], (LANES - 2 + row_off) % LANES, 1)
        last = last + pltpu.roll(outer[low : low + channels, LANES:], (LANES - 2 + row_off) % LANES, 1)
    for place in range(0, height + 2, 2):
        if place == 0:
            cells = jnp.concatenate([top[...], grads[:, :LANES]], 1)
        elif place == height:
            cells = jnp.concatenate([grads[:, (height - 1) * LANES :], bottom[...]], 1)
        else:
            cells = grads[:, (place - 1) * LANES : (place + 1) * LANES]
        product = jnp.dot(weights[...], cells, preferred_element_type=F32)
        for half in range(2):
            for row_off in range(3):
                n = place + half - 1 + row_off - 1
                if not 0 <= n < height:
                    continue
                for col_off in range(3):
                    start = (3 * row_off + col_off) * channels
                    piece = product[start : start + channels, half * LANES : (half + 1) * LANES]
                    if row_off == 2 or (place + half == 0):
                        sums[n, col_off] = piece
                    else:
                        sums[n, col_off] = sums[n, col_off] + piece
    for n in range(height):
        total = sums[n, 1]
        total = total + jnp.where(
            lane == LANES - 1, pltpu.roll(last, LANES - 1 - n, 1), pltpu.roll(sums[n, 0], LANES - 1, 1)
        )
        total = total + jnp.where(
            lane == 0, pltpu.roll(first, (LANES - n) % LANES, 1), pltpu.roll(sums[n, 2], 1, 1)
        )
        rows[pl.ds(n, channels, stride=height), :] = total
    grad_frame[...] = rows[: inputs * height].astype(BF16)
    grad_hidden_prev[...] = rows[inputs * height :].astype(BF16)


def finish_kernel(total, kernel_step, bias_step):
    block = kernel_step.shape[0] // 3
    parts = [total[i * STACK : i * STACK + block].astype(F32) for i in range(3)]
    bias_grad = total[block : block + 8].astype(F32)[:1]
    norm = jnp.sqrt(sum(jnp.sum(part * part) for part in parts) + jnp.sum(bias_grad * bias_grad))
    factor = jnp.minimum(1.0, CLIP_NORM / norm)
    for i, part in enumerate(parts):
        kernel_step[i * block : (i + 1) * block] = part * factor
    bias_step[...] = bias_grad * factor


def sum_kernel(parts, *rest):
    copies = rest[-1]
    total = jnp.sum(parts[...].astype(F32), 0).astype(copies.dtype)
    copies[...] = jnp.broadcast_to(total[None], copies.shape)


def summed(parts, copies, kind, *after):
    return pl.pallas_call(
        sum_kernel,
        out_shape=jax.ShapeDtypeStruct((copies,) + parts.shape[1:], kind),
        in_specs=vmem(1) + [pl.BlockSpec(memory_space=pl.ANY)] * len(after),
        out_specs=vmem(1)[0],
        compiler_params=pltpu.CompilerParams(vmem_limit_bytes=8 * 2**20),
    )(parts, *after)


def exchanged(copies, axes):
    return lax.all_to_all(copies, axes, 0, 0, tiled=True)


def end_columns(top, low, high, bottom):
    spare = ((0, 0), (0, LANES - low.shape[1] - 2))
    return (
        jnp.pad(jnp.concatenate([top[:, :1], low, bottom[:, :1]], 1), spare),
        jnp.pad(jnp.concatenate([top[:, -1:], high, bottom[:, -1:]], 1), spare),
    )


def shape(rows, columns, kind):
    return jax.ShapeDtypeStruct((rows, columns), kind)


def per_device(frame, hidden_prev, cell_prev, kernel, bias, grad_hidden, grad_cell):
    inputs, height, breadth = frame.shape
    units = hidden_prev.shape[0]
    channels = inputs + units
    gate_rows = kernel.shape[0]
    cells = height * breadth
    row = jnp.concatenate([frame[:, 0], hidden_prev[:, 0]], 0)
    last_row = jnp.concatenate([frame[:, -1], hidden_prev[:, -1]], 0)
    column = jnp.concatenate([frame[:, :, 0], hidden_prev[:, :, 0]], 0)
    last_column = jnp.concatenate([frame[:, :, -1], hidden_prev[:, :, -1]], 0)
    weights = kernel.reshape(gate_rows, 3, 3 * channels)
    weights = jnp.pad(weights, ((0, 0), (0, 0), (0, STACK - 3 * channels))).reshape(gate_rows, 3 * STACK)
    weights_back = kernel.T
    top, bottom = neighbours(row, last_row, NS)
    left, right = neighbours(*end_columns(top, column, last_column, bottom), EW)

    hidden, cell, grad_cell_prev, grads, edges, terms = pl.pallas_call(
        forward_kernel,
        out_shape=(
            shape(units * height, breadth, BF16),
            shape(units * height, breadth, F32),
            shape(units * height, breadth, F32),
            shape(gate_rows, cells, BF16),
            shape(gate_rows, LANES, BF16),
            shape(3 * STACK, gate_rows, BF16),
        ),
        in_specs=vmem(11),
        out_specs=tuple(vmem(6)),
        scratch_shapes=[
            pltpu.VMEM((channels * height, breadth), F32),
            pltpu.VMEM((STACK, (height + 2) * breadth), BF16),
            pltpu.VMEM((units * height, breadth), F32),
        ],
        compiler_params=pltpu.CompilerParams(vmem_limit_bytes=16 * 2**20),
        cost_estimate=pl.CostEstimate(flops=1_400_000_000, bytes_accessed=6_000_000, transcendentals=700_000),
    )(
        frame.reshape(inputs * height, breadth),
        hidden_prev.reshape(units * height, breadth),
        top,
        bottom,
        left,
        right,
        weights,
        bias[:, None],
        cell_prev.reshape(units * height, breadth),
        grad_hidden.reshape(units * height, breadth),
        grad_cell.reshape(units * height, breadth),
    )

    plane = lax.axis_size(PLANE)
    low, high = lax.axis_size("z_lo"), lax.axis_size("z_hi")
    mine = exchanged(terms.reshape(plane, -1, gate_rows), PLANE)
    grad_top, grad_bottom = neighbours(grads[:, :LANES], grads[:, cells - LANES :], NS)
    mine = exchanged(summed(mine, low, F32, grad_top, grad_bottom), "z_lo")
    mine = exchanged(summed(mine, high, F32), "z_hi")
    grad_left, grad_right = neighbours(
        *end_columns(grad_top, edges[:, :height], edges[:, height : 2 * height], grad_bottom), EW
    )
    mine = summed(mine, plane, BF16, grad_left, grad_right)
    total = exchanged(mine, PLANE).reshape(3 * STACK, gate_rows)
    grad_frame, grad_hidden_prev = pl.pallas_call(
        backward_kernel,
        out_shape=(shape(inputs * height, breadth, BF16), shape(units * height, breadth, BF16)),
        in_specs=vmem(6),
        out_specs=tuple(vmem(2)),
        scratch_shapes=[
            pltpu.VMEM((height, 3, channels, breadth), F32),
            pltpu.VMEM((channels * height, breadth), F32),
        ],
        compiler_params=pltpu.CompilerParams(vmem_limit_bytes=16 * 2**20),
        cost_estimate=pl.CostEstimate(flops=764_000_000, bytes_accessed=3_000_000, transcendentals=0),
    )(weights_back, grads, grad_top, grad_bottom, grad_left, grad_right)
    kernel_step, bias_step = pl.pallas_call(
        finish_kernel,
        out_shape=(shape(9 * channels, gate_rows, F32), shape(1, gate_rows, F32)),
        in_specs=vmem(1),
        out_specs=tuple(vmem(2)),
        compiler_params=pltpu.CompilerParams(vmem_limit_bytes=16 * 2**20),
    )(total)
    whole = (units, height, breadth)
    return (
        hidden.reshape(whole),
        cell.reshape(whole),
        grad_frame.reshape(frame.shape),
        grad_hidden_prev.reshape(whole),
        grad_cell_prev.reshape(whole),
        kernel_step.T,
        bias_step.reshape(gate_rows),
    )


def solution(mesh):
    mesh = Mesh(mesh.devices.reshape(4, 4, 2, 4, 2, 2), EW + NS)
    grid = P(None, NS, EW)
    return jax.shard_map(
        per_device,
        mesh=mesh,
        in_specs=(grid, grid, grid, P(), P(), grid, grid),
        out_specs=(grid, grid, grid, grid, grid, P(), P()),
        check_vma=False,
    )
```

```python
import functools

import jax
import jax.numpy as jnp
from jax import lax
from jax.experimental import pallas as pl
from jax.experimental.pallas import tpu as pltpu
from jax.sharding import Mesh, PartitionSpec as P

CLIP_NORM = 100.0
EW = ("z_hi", "z_lo", "x_hi")
NS = ("y", "x_lo", "core")
PLANE = ("x_hi", "y", "x_lo", "core")
LANES = 128
STACK = 256
BF16 = jnp.bfloat16
F32 = jnp.float32


def vmem(count):
    return [pl.BlockSpec(memory_space=pltpu.VMEM)] * count


def neighbours(to_before, to_after, axes):
    count = lax.axis_size(axes)
    forward = [(i, i + 1) for i in range(count - 1)]
    backward = [(target, source) for source, target in forward]
    return lax.ppermute(to_after, axes, forward), lax.ppermute(to_before, axes, backward)


def sigmoid(x):
    return 0.5 * jnp.tanh(0.5 * x) + 0.5


def rows_kernel(frame, hidden_prev, cell_prev, grad_hidden, grad_cell, joined, up, down, *, height):
    inputs = frame.shape[0]
    joined[:inputs] = frame[...].astype(F32)
    joined[inputs:] = hidden_prev[...].astype(F32)
    channels = joined.shape[0] // height
    units = cell_prev.shape[0] // height
    for out, rows, state_row in ((up, (0, 1), 0), (down, (height - 2, height - 1), height - 1)):
        for i, n in enumerate(rows):
            out[i * channels : (i + 1) * channels] = joined[pl.ds(n, channels, stride=height), :]
        for i, state in enumerate((cell_prev, grad_hidden, grad_cell)):
            start = 2 * channels + i * units
            out[start : start + units] = state[pl.ds(state_row, units, stride=height), :]


def put_channels(tile, row, place):
    lane = lax.broadcasted_iota(jnp.int32, tile.shape, 1)
    return jnp.where(lane // 4 == place, pltpu.roll(row, (4 * place + 2) % LANES, 1), tile)


def put_state(tile, row, place, slot):
    lane = lax.broadcasted_iota(jnp.int32, tile.shape, 1)
    return jnp.where(lane // 2 == 2 * place + slot // 2, pltpu.roll(row, (4 * place + slot + 1) % LANES, 1), tile)


def columns_kernel(joined, cell_prev, grad_hidden, grad_cell, columns, *, height):
    channels = joined.shape[0] // height
    units = cell_prev.shape[0] // height
    tile = jnp.zeros((channels, LANES), F32)
    pairs = jnp.zeros((units, LANES), F32)
    single = jnp.zeros((units, LANES), F32)
    for n in range(height):
        at = pl.ds(n, units, stride=height)
        tile = put_channels(tile, joined[pl.ds(n, channels, stride=height), :], n + 2)
        pairs = put_state(pairs, cell_prev[at, :], n + 1, 0)
        pairs = put_state(pairs, grad_hidden[at, :], n + 1, 2)
        single = put_state(single, grad_cell[at, :], n + 1, 0)
    columns[:channels] = tile
    columns[channels : channels + units] = pairs
    columns[channels + units :] = single


def corners_kernel(columns, top, bottom, out, *, height, units):
    channels = columns.shape[0] - 2 * units
    tile = columns[:channels]
    pairs = columns[channels : channels + units]
    single = columns[channels + units :]
    for rows, place, state_place in ((top, 0, 0), (bottom, height + 2, height + 1)):
        for i in range(2):
            tile = put_channels(tile, rows[i * channels : (i + 1) * channels], place + i)
        states = [rows[2 * channels + i * units : 2 * channels + (i + 1) * units] for i in range(3)]
        pairs = put_state(pairs, states[0], state_place, 0)
        pairs = put_state(pairs, states[1], state_place, 2)
        single = put_state(single, states[2], state_place, 0)
    out[:channels] = tile
    out[channels : channels + units] = pairs
    out[channels + units :] = single


def gate_step(gates, old, down, grad_cell):
    units = old.shape[0]
    input_gate = sigmoid(gates[:units])
    forget_gate = sigmoid(gates[units : 2 * units])
    cand_gate = jnp.tanh(gates[2 * units : 3 * units])
    output_gate = sigmoid(gates[3 * units :])
    new = forget_gate * old + input_gate * cand_gate
    new_tanh = jnp.tanh(new)
    cell_grad = grad_cell + down * output_gate * (1.0 - new_tanh * new_tanh)
    grads = jnp.concatenate(
        [
            cell_grad * cand_gate * input_gate * (1.0 - input_gate),
            cell_grad * old * forget_gate * (1.0 - forget_gate),
            cell_grad * input_gate * (1.0 - cand_gate * cand_gate),
            down * new_tanh * output_gate * (1.0 - output_gate),
        ],
        0,
    ).astype(BF16)
    return output_gate * new_tanh, new, cell_grad * forget_gate, grads


def forward_kernel(
    joined, columns, left, right, top, bottom, weights, bias, cell_prev, grad_hidden, grad_cell,
    hidden, cell, grad_cell_prev, grads, side_grads, terms,
    stacked, hidden_rows,
):
    units = bias.shape[0] // 4
    height = cell_prev.shape[0] // units
    channels = joined.shape[0] // height
    lane = lax.broadcasted_iota(jnp.int32, (channels, LANES), 1)
    spare = STACK - 3 * channels
    ones_row = (lax.broadcasted_iota(jnp.int32, (spare, LANES), 0) == 0).astype(F32)
    own = columns[:channels]
    outer = jnp.where(lane % 4 < 2, left[:channels], right[:channels])
    for place in range(height + 4):
        if place < 2:
            row = top[place * channels : (place + 1) * channels]
        elif place >= height + 2:
            row = bottom[(place - height - 2) * channels : (place - height - 1) * channels]
        else:
            row = joined[pl.ds(place - 2, channels, stride=height), :]
        west = pltpu.roll(outer, (LANES - 4 * place - 1) % LANES, 1)
        east = pltpu.roll(outer, (LANES - 4 * place - 3) % LANES, 1)
        before = jnp.where(lane == 0, west, pltpu.roll(row, 1, 1))
        after = jnp.where(lane == LANES - 1, east, pltpu.roll(row, LANES - 1, 1))
        stacked[:, place * LANES : (place + 1) * LANES] = jnp.concatenate([before, row, after, ones_row], 0).astype(
            BF16
        )
    bias_cells = jnp.broadcast_to(bias[...], (4 * units, LANES))

    side = jnp.concatenate(
        [
            jnp.where(lane % 4 == 0, outer, own),
            pltpu.roll(outer, LANES - 1, 1),
            pltpu.roll(jnp.where(lane % 4 == 2, own, outer), LANES - 2, 1),
        ],
        0,
    )
    gates = bias_cells
    for row_off in range(3):
        moved = pltpu.roll(side, LANES - 4 * row_off, 1) if row_off else side
        gates = gates + jnp.dot(
            weights[:, row_off * STACK : (row_off + 1) * STACK],
            jnp.concatenate([moved, ones_row], 0).astype(BF16),
            preferred_element_type=F32,
        )
    lane = lax.broadcasted_iota(jnp.int32, (units, LANES), 1)
    pairs = slice(channels, channels + units)
    single = slice(channels + units, channels + 2 * units)
    pairs = jnp.where(lane % 2 == 0, left[pairs], right[pairs])
    single = jnp.where(lane % 2 == 0, left[single], right[single])
    side_grads[...] = gate_step(gates, pairs, pltpu.roll(pairs, LANES - 2, 1), single)[3]

    for pair in range(height // 2 + 1):
        sums = jnp.zeros((4 * units, 2 * LANES), F32)
        for row_off in range(3):
            start = (2 * pair + row_off) * LANES
            sums = sums + jnp.dot(
                weights[:, row_off * STACK : (row_off + 1) * STACK],
                stacked[:, start : start + 2 * LANES],
                preferred_element_type=F32,
            )
        for half in range(2):
            place = 2 * pair + half
            gates = sums[:, half * LANES : (half + 1) * LANES] + bias_cells
            inside = 0 < place <= height
            if inside:
                at = pl.ds(place - 1, units, stride=height)
                states = [cell_prev[at, :], grad_hidden[at, :], grad_cell[at, :]]
            else:
                rows = bottom if place else top
                states = [rows[2 * channels + i * units : 2 * channels + (i + 1) * units] for i in range(3)]
            new_hidden, new, down, row_grads = gate_step(gates, *states)
            grads[:, place * LANES : (place + 1) * LANES] = row_grads
            if inside:
                hidden_rows[at, :] = new_hidden
                cell[at, :] = new
                grad_cell_prev[at, :] = down
    hidden[...] = hidden_rows[...].astype(BF16)
    for row_off in range(3):
        terms[row_off * STACK : (row_off + 1) * STACK] = lax.dot_general(
            stacked[:, (row_off + 1) * LANES : (row_off + 1 + height) * LANES],
            grads[:, LANES : (height + 1) * LANES],
            (((1,), (1,)), ((), ())),
            preferred_element_type=F32,
        ).astype(BF16)


def backward_kernel(weights, grads, side_grads, grad_frame, grad_hidden_prev, sums, rows):
    height = grads.shape[1] // LANES - 2
    inputs = grad_frame.shape[0] // height
    channels = rows.shape[0] // height
    lane = lax.broadcasted_iota(jnp.int32, (channels, LANES), 1)
    outer = jnp.dot(weights[...], side_grads[...], preferred_element_type=F32)
    first = jnp.zeros((channels, LANES), F32)
    last = jnp.zeros((channels, LANES), F32)
    for row_off in range(3):
        low, high = 3 * row_off * channels, (3 * row_off + 2) * channels
        back = (LANES - 4 * (2 - row_off)) % LANES
        first = first + pltpu.roll(outer[high : high + channels], back, 1)
        last = last + pltpu.roll(outer[low : low + channels], back, 1)
    for place in range(0, height + 2, 2):
        cells = grads[:, place * LANES : (place + 2) * LANES]
        product = jnp.dot(weights[...], cells, preferred_element_type=F32)
        for half in range(2):
            for row_off in range(3):
                n = place + half + row_off - 2
                if not 0 <= n < height:
                    continue
                for col_off in range(3):
                    start = (3 * row_off + col_off) * channels
                    piece = product[start : start + channels, half * LANES : (half + 1) * LANES]
                    if row_off == 2:
                        sums[n, col_off] = piece
                    else:
                        sums[n, col_off] = sums[n, col_off] + piece
    for n in range(height):
        west = pltpu.roll(first, (LANES - 4 * n) % LANES, 1)
        east = pltpu.roll(last, LANES - 2 - 4 * n, 1)
        total = sums[n, 1]
        total = total + jnp.where(lane == LANES - 1, east, pltpu.roll(sums[n, 0], LANES - 1, 1))
        total = total + jnp.where(lane == 0, west, pltpu.roll(sums[n, 2], 1, 1))
        rows[pl.ds(n, channels, stride=height), :] = total
    grad_frame[...] = rows[: inputs * height].astype(BF16)
    grad_hidden_prev[...] = rows[inputs * height :].astype(BF16)


def finish_kernel(total, kernel_step, bias_step):
    block = kernel_step.shape[0] // 3
    parts = [total[i * STACK : i * STACK + block].astype(F32) for i in range(3)]
    bias_grad = total[block : block + 8].astype(F32)[:1]
    norm = jnp.sqrt(sum(jnp.sum(part * part) for part in parts) + jnp.sum(bias_grad * bias_grad))
    factor = jnp.minimum(1.0, CLIP_NORM / norm)
    for i, part in enumerate(parts):
        kernel_step[i * block : (i + 1) * block] = part * factor
    bias_step[...] = bias_grad * factor


def sum_kernel(parts, *rest):
    copies = rest[-1]
    total = jnp.sum(parts[...].astype(F32), 0).astype(copies.dtype)
    copies[...] = jnp.broadcast_to(total[None], copies.shape)


def summed(parts, copies, kind, *after):
    return pl.pallas_call(
        sum_kernel,
        out_shape=jax.ShapeDtypeStruct((copies,) + parts.shape[1:], kind),
        in_specs=vmem(1) + [pl.BlockSpec(memory_space=pl.ANY)] * len(after),
        out_specs=vmem(1)[0],
        compiler_params=pltpu.CompilerParams(vmem_limit_bytes=8 * 2**20),
    )(parts, *after)


def exchanged(copies, axes):
    return lax.all_to_all(copies, axes, 0, 0, tiled=True)


def shape(rows, columns, kind):
    return jax.ShapeDtypeStruct((rows, columns), kind)


def called(kernel, outs, scratch, cost, *args, mebibytes=16):
    return pl.pallas_call(
        kernel,
        out_shape=tuple(outs),
        in_specs=vmem(len(args)),
        out_specs=tuple(vmem(len(outs))),
        scratch_shapes=scratch,
        compiler_params=pltpu.CompilerParams(vmem_limit_bytes=mebibytes * 2**20),
        cost_estimate=pl.CostEstimate(flops=cost, bytes_accessed=2 * cost // 1000, transcendentals=0),
    )(*args)


def per_device(frame, hidden_prev, cell_prev, kernel, bias, grad_hidden, grad_cell):
    inputs, height, breadth = frame.shape
    units = hidden_prev.shape[0]
    channels = inputs + units
    gate_rows = kernel.shape[0]
    weights = kernel.reshape(gate_rows, 3, 3 * channels)
    weights = jnp.pad(weights, ((0, 0), (0, 0), (0, STACK - 3 * channels))).reshape(gate_rows, 3 * STACK)
    flat = (units * height, breadth)
    states = (cell_prev.reshape(flat), grad_hidden.reshape(flat), grad_cell.reshape(flat))

    strip = shape(2 * channels + 3 * units, breadth, F32)
    joined, up, down = called(
        functools.partial(rows_kernel, height=height),
        [shape(channels * height, breadth, F32), strip, strip],
        [],
        1_000_000,
        frame.reshape(inputs * height, breadth),
        hidden_prev.reshape(flat),
        *states,
    )
    edge = shape(channels + 2 * units, LANES, F32)
    (columns,) = called(functools.partial(columns_kernel, height=height), [edge], [], 1_000_000, joined, *states)
    top, bottom = neighbours(up, down, NS)
    (columns,) = called(functools.partial(corners_kernel, height=height, units=units), [edge], [], 100_000, columns, top, bottom)
    left, right = neighbours(columns, columns, EW)

    hidden, cell, grad_cell_prev, grads, side_grads, terms = called(
        forward_kernel,
        [
            shape(*flat, BF16),
            shape(*flat, F32),
            shape(*flat, F32),
            shape(gate_rows, (height + 2) * breadth, BF16),
            shape(gate_rows, LANES, BF16),
            shape(3 * STACK, gate_rows, BF16),
        ],
        [pltpu.VMEM((STACK, (height + 4) * breadth), BF16), pltpu.VMEM(flat, F32)],
        1_400_000_000,
        joined,
        columns,
        left,
        right,
        top,
        bottom,
        weights,
        bias[:, None],
        *states,
    )

    plane = lax.axis_size(PLANE)
    low, high = lax.axis_size("z_lo"), lax.axis_size("z_hi")
    mine = exchanged(terms.reshape(plane, -1, gate_rows), PLANE)
    mine = exchanged(summed(mine, low, F32), "z_lo")
    mine = exchanged(summed(mine, high, F32), "z_hi")
    mine = summed(mine, plane, BF16)
    total = exchanged(mine, PLANE).reshape(3 * STACK, gate_rows)
    grad_frame, grad_hidden_prev = called(
        backward_kernel,
        [shape(inputs * height, breadth, BF16), shape(*flat, BF16)],
        [pltpu.VMEM((height, 3, channels, breadth), F32), pltpu.VMEM((channels * height, breadth), F32)],
        764_000_000,
        kernel.T,
        grads,
        side_grads,
    )
    kernel_step, bias_step = called(
        finish_kernel, [shape(9 * channels, gate_rows, F32), shape(1, gate_rows, F32)], [], 1_000_000, total
    )
    whole = (units, height, breadth)
    return (
        hidden.reshape(whole),
        cell.reshape(whole),
        grad_frame.reshape(frame.shape),
        grad_hidden_prev.reshape(whole),
        grad_cell_prev.reshape(whole),
        kernel_step.T,
        bias_step.reshape(gate_rows),
    )


def solution(mesh):
    mesh = Mesh(mesh.devices.reshape(4, 4, 2, 4, 2, 2), EW + NS)
    grid = P(None, NS, EW)
    return jax.shard_map(
        per_device,
        mesh=mesh,
        in_specs=(grid, grid, grid, P(), P(), grid, grid),
        out_specs=(grid, grid, grid, grid, grid, P(), P()),
        check_vma=False,
    )
```

```python
import functools

import jax
import jax.numpy as jnp
from jax import lax
from jax.experimental import pallas as pl
from jax.experimental.pallas import tpu as pltpu
from jax.sharding import Mesh, PartitionSpec as P

CLIP_NORM = 100.0
EW = ("z_hi", "z_lo", "x_hi")
NS = ("y", "x_lo", "core")
PLANE = ("x_hi", "y", "x_lo", "core")
LANES = 128
STACK = 256
BF16 = jnp.bfloat16
F32 = jnp.float32


def vmem(count):
    return [pl.BlockSpec(memory_space=pltpu.VMEM)] * count


def neighbours(to_before, to_after, axes):
    count = lax.axis_size(axes)
    forward = [(i, i + 1) for i in range(count - 1)]
    backward = [(target, source) for source, target in forward]
    return lax.ppermute(to_after, axes, forward), lax.ppermute(to_before, axes, backward)


def sigmoid(x):
    return 0.5 * jnp.tanh(0.5 * x) + 0.5


def rows_kernel(
    frame, hidden_prev, cell_prev, grad_hidden, grad_cell, up, down, joined, frame_here, hidden_here, *rest, height
):
    *here, sems = rest
    copies = [
        pltpu.make_async_copy(source, target, sems.at[i])
        for i, (source, target) in enumerate(
            zip((frame, hidden_prev, cell_prev, grad_hidden, grad_cell), (frame_here, hidden_here, *here))
        )
    ]
    for copy in copies:
        copy.start()
    inputs = frame_here.shape[0]
    channels = joined.shape[0] // height
    units = here[0].shape[0] // height
    sides = ((up, (0, 1), 0), (down, (height - 2, height - 1), height - 1))
    copies[0].wait()
    joined[:inputs] = frame_here[...].astype(F32)
    copies[1].wait()
    joined[inputs:] = hidden_here[...].astype(F32)
    for out, rows, _ in sides:
        for i, n in enumerate(rows):
            out[i * channels : (i + 1) * channels] = joined[pl.ds(n, channels, stride=height), :]
    for i, state in enumerate(here):
        copies[2 + i].wait()
        start = 2 * channels + i * units
        for out, _, n in sides:
            out[start : start + units] = state[pl.ds(n, units, stride=height), :]


def put_channels(tile, row, place):
    lane = lax.broadcasted_iota(jnp.int32, tile.shape, 1)
    return jnp.where(lane // 4 == place, pltpu.roll(row, (4 * place + 2) % LANES, 1), tile)


def put_state(tile, row, place, slot):
    lane = lax.broadcasted_iota(jnp.int32, tile.shape, 1)
    return jnp.where(lane // 2 == 2 * place + slot // 2, pltpu.roll(row, (4 * place + slot + 1) % LANES, 1), tile)


def columns_kernel(
    frame, hidden_prev, cell_prev, grad_hidden, grad_cell, kernel, columns, weights, joined, *, height
):
    joined[: frame.shape[0]] = frame[...].astype(F32)
    joined[frame.shape[0] :] = hidden_prev[...].astype(F32)
    depth = kernel.shape[0] // 3
    blank = jnp.zeros((STACK - depth, kernel.shape[1]), F32)
    for row_off in range(3):
        part = kernel[...].astype(F32)[row_off * depth : (row_off + 1) * depth]
        weights[:, row_off * STACK : (row_off + 1) * STACK] = jnp.concatenate([part, blank], 0).T.astype(BF16)
    channels = joined.shape[0] // height
    units = cell_prev.shape[0] // height
    tile = jnp.zeros((channels, LANES), F32)
    pairs = jnp.zeros((units, LANES), F32)
    single = jnp.zeros((units, LANES), F32)
    for n in range(height):
        at = pl.ds(n, units, stride=height)
        tile = put_channels(tile, joined[pl.ds(n, channels, stride=height), :], n + 2)
        pairs = put_state(pairs, cell_prev[at, :], n + 1, 0)
        pairs = put_state(pairs, grad_hidden[at, :], n + 1, 2)
        single = put_state(single, grad_cell[at, :], n + 1, 0)
    columns[:channels] = tile
    columns[channels : channels + units] = pairs
    columns[channels + units :] = single


def corners_kernel(columns, top, bottom, out, *, height, units):
    channels = columns.shape[0] - 2 * units
    tile = columns[:channels]
    pairs = columns[channels : channels + units]
    single = columns[channels + units :]
    for rows, place, state_place in ((top, 0, 0), (bottom, height + 2, height + 1)):
        for i in range(2):
            tile = put_channels(tile, rows[i * channels : (i + 1) * channels], place + i)
        states = [rows[2 * channels + i * units : 2 * channels + (i + 1) * units] for i in range(3)]
        pairs = put_state(pairs, states[0], state_place, 0)
        pairs = put_state(pairs, states[1], state_place, 2)
        single = put_state(single, states[2], state_place, 0)
    out[:channels] = tile
    out[channels : channels + units] = pairs
    out[channels + units :] = single


def gate_step(gates, old, down, grad_cell):
    units = old.shape[0]
    input_gate = sigmoid(gates[:units])
    forget_gate = sigmoid(gates[units : 2 * units])
    cand_gate = jnp.tanh(gates[2 * units : 3 * units])
    output_gate = sigmoid(gates[3 * units :])
    new = forget_gate * old + input_gate * cand_gate
    new_tanh = jnp.tanh(new)
    cell_grad = grad_cell + down * output_gate * (1.0 - new_tanh * new_tanh)
    grads = [
        cell_grad * cand_gate * input_gate * (1.0 - input_gate),
        cell_grad * old * forget_gate * (1.0 - forget_gate),
        cell_grad * input_gate * (1.0 - cand_gate * cand_gate),
        down * new_tanh * output_gate * (1.0 - output_gate),
    ]
    return output_gate * new_tanh, new, cell_grad * forget_gate, jnp.concatenate(grads, 0)


def forward_kernel(
    joined, top, bottom, weights, bias, cell_prev, grad_hidden, grad_cell,
    hidden, cell, grad_cell_prev, grads, terms,
    stacked,
):
    units = bias.shape[0] // 4
    height = cell_prev.shape[0] // units
    channels = joined.shape[0] // height
    spare = STACK - 3 * channels
    ones_row = (lax.broadcasted_iota(jnp.int32, (spare, LANES), 0) == 0).astype(F32)
    for place in range(height + 4):
        if place < 2:
            row = top[place * channels : (place + 1) * channels]
        elif place >= height + 2:
            row = bottom[(place - height - 2) * channels : (place - height - 1) * channels]
        else:
            row = joined[pl.ds(place - 2, channels, stride=height), :]
        stacked[:, place * LANES : (place + 1) * LANES] = jnp.concatenate(
            [pltpu.roll(row, 1, 1), row, pltpu.roll(row, LANES - 1, 1), ones_row], 0
        ).astype(BF16)
    bias_cells = jnp.broadcast_to(bias[...], (4 * units, LANES))
    lane = lax.broadcasted_iota(jnp.int32, (4 * units, LANES), 1)
    middle = (lane > 0) & (lane < LANES - 1)
    for pair in range(height // 2 + 1):
        sums = jnp.zeros((4 * units, 2 * LANES), F32)
        for row_off in range(3):
            start = (2 * pair + row_off) * LANES
            sums = sums + jnp.dot(
                weights[:, row_off * STACK : (row_off + 1) * STACK],
                stacked[:, start : start + 2 * LANES],
                preferred_element_type=F32,
            )
        for half in range(2):
            place = 2 * pair + half
            gates = sums[:, half * LANES : (half + 1) * LANES] + bias_cells
            inside = 0 < place <= height
            if inside:
                at = pl.ds(place - 1, units, stride=height)
                states = [cell_prev[at, :], grad_hidden[at, :], grad_cell[at, :]]
            else:
                rows = bottom if place else top
                states = [rows[2 * channels + i * units : 2 * channels + (i + 1) * units] for i in range(3)]
            new_hidden, new, down, row_grads = gate_step(gates, *states)
            grads[:, place * LANES : (place + 1) * LANES] = jnp.where(middle, row_grads, 0.0).astype(BF16)
            if inside:
                hidden[at, :] = new_hidden
                cell[at, :] = new
                grad_cell_prev[at, :] = down
    for row_off in range(3):
        terms[row_off * STACK : (row_off + 1) * STACK] = lax.dot_general(
            stacked[:, (row_off + 1) * LANES : (row_off + 1 + height) * LANES],
            grads[:, LANES : (height + 1) * LANES],
            (((1,), (1,)), ((), ())),
            preferred_element_type=F32,
        )


def sides_kernel(columns, left, right, weights, bias, inner_terms, side_grads, side_cells, terms, *, height):
    units = bias.shape[0] // 4
    channels = columns.shape[0] - 2 * units
    spare = STACK - 3 * channels

    def moved(x, lanes):
        return pltpu.roll(x, lanes % LANES, 1)

    slot = lax.broadcasted_iota(jnp.int32, (channels, LANES), 1) % 4
    own = columns[:channels]
    outer = jnp.where(slot < 2, left[:channels], right[:channels])
    before = jnp.where(
        slot == 0, outer, jnp.where(slot == 1, moved(own, 1), jnp.where(slot == 2, moved(outer, 1), moved(own, 2)))
    )
    at = jnp.where(slot == 0, moved(outer, -1), jnp.where(slot == 3, moved(outer, 1), own))
    after = jnp.where(
        slot == 0, moved(own, -2), jnp.where(slot == 1, moved(outer, -1), jnp.where(slot == 2, moved(own, -1), outer))
    )
    patches = jnp.concatenate([before, at, after], 0)
    ones_row = (lax.broadcasted_iota(jnp.int32, (spare, LANES), 0) == 0).astype(F32)
    stacks = [
        jnp.concatenate([moved(patches, -4 * row_off) if row_off else patches, ones_row], 0).astype(BF16)
        for row_off in range(3)
    ]
    gates = jnp.broadcast_to(bias[...], (4 * units, LANES))
    for row_off in range(3):
        gates = gates + jnp.dot(
            weights[:, row_off * STACK : (row_off + 1) * STACK], stacks[row_off], preferred_element_type=F32
        )
    slot = slot[:units]
    rows = slice(channels, channels + units)
    here, west, east = columns[rows], left[rows], right[rows]
    old = jnp.where(slot == 0, west, jnp.where(slot == 3, moved(east, 2), moved(here, 1)))
    down = jnp.where(slot == 0, moved(west, -2), jnp.where(slot == 3, east, moved(here, -1)))
    rows = slice(channels + units, channels + 2 * units)
    here, west, east = columns[rows], left[rows], right[rows]
    grad_cell = jnp.where(slot == 0, west, jnp.where(slot == 3, moved(east, 2), moved(here, 1)))
    new_hidden, new, back, grads = gate_step(gates, old, down, grad_cell)
    side_cells[:units] = new_hidden
    side_cells[units : 2 * units] = new
    side_cells[2 * units :] = back
    side_grads[...] = grads.astype(BF16)
    lane = lax.broadcasted_iota(jnp.int32, grads.shape, 1)
    inside = (lane >= 4) & (lane < 4 * (height + 1)) & ((lane % 4 == 1) | (lane % 4 == 2))
    grads = jnp.where(inside, grads, 0.0).astype(BF16)
    for row_off in range(3):
        part = slice(row_off * STACK, (row_off + 1) * STACK)
        terms[part] = (
            inner_terms[part]
            + lax.dot_general(
                stacks[row_off], grads, (((1,), (1,)), ((), ())), preferred_element_type=F32
            )
        ).astype(BF16)


def backward_kernel(
    weights, grads, side_grads, side_cells, inner_hidden, inner_cell, inner_back,
    hidden, cell, grad_cell_prev, grad_frame, grad_hidden_prev,
    sums, rows,
):
    height = grads.shape[1] // LANES - 2
    units = hidden.shape[0] // height
    inputs = grad_frame.shape[0] // height
    channels = inputs + units
    lane = lax.broadcasted_iota(jnp.int32, (channels, LANES), 1)
    ends = (lane[:units] == 0) | (lane[:units] == LANES - 1)
    for n in range(height):
        at = pl.ds(n, units, stride=height)
        for i, (inner, out) in enumerate(((inner_hidden, rows), (inner_cell, cell), (inner_back, grad_cell_prev))):
            side = pltpu.roll(side_cells[i * units : (i + 1) * units], LANES - 4 * (n + 1) - 2, 1)
            out[at, :] = jnp.where(ends, side, inner[at, :])
    hidden[...] = rows[: units * height].astype(BF16)

    outer = jnp.dot(weights[...], side_grads[...], preferred_element_type=F32)
    parts = []
    for col_off in range(3):
        part = jnp.zeros((channels, LANES), F32)
        for row_off in range(3):
            start = (3 * row_off + col_off) * channels
            piece = outer[start : start + channels]
            part = part + (pltpu.roll(piece, LANES - 4 * (2 - row_off), 1) if row_off < 2 else piece)
        parts.append(part)
    slot = lane % 4
    sides = jnp.where((slot == 1) | (slot == 2), parts[1], 0.0) + jnp.where(
        slot == 0,
        pltpu.roll(parts[0], LANES - 1, 1),
        jnp.where(
            slot == 1,
            pltpu.roll(parts[0], LANES - 2, 1),
            jnp.where(slot == 2, pltpu.roll(parts[2], 2, 1), pltpu.roll(parts[2], 1, 1)),
        ),
    )
    for place in range(0, height + 2, 2):
        cells = grads[:, place * LANES : (place + 2) * LANES]
        product = jnp.dot(weights[...], cells, preferred_element_type=F32)
        for half in range(2):
            for row_off in range(3):
                n = place + half + row_off - 2
                if not 0 <= n < height:
                    continue
                for col_off in range(3):
                    start = (3 * row_off + col_off) * channels
                    piece = product[start : start + channels, half * LANES : (half + 1) * LANES]
                    if row_off == 2:
                        sums[n, col_off] = piece
                    else:
                        sums[n, col_off] = sums[n, col_off] + piece
    edge = (lane < 2) | (lane >= LANES - 2)
    for n in range(height):
        total = sums[n, 1] + pltpu.roll(sums[n, 0], LANES - 1, 1) + pltpu.roll(sums[n, 2], 1, 1)
        total = total + jnp.where(edge, pltpu.roll(sides, LANES - 4 * n - 2, 1), 0.0)
        rows[pl.ds(n, channels, stride=height), :] = total
    grad_frame[...] = rows[: inputs * height].astype(BF16)
    grad_hidden_prev[...] = rows[inputs * height :].astype(BF16)


def finish_kernel(total, kernel_step, bias_step):
    block = kernel_step.shape[0] // 3
    parts = [total[i * STACK : i * STACK + block].astype(F32) for i in range(3)]
    bias_grad = total[block : block + 8].astype(F32)[:1]
    norm = jnp.sqrt(sum(jnp.sum(part * part) for part in parts) + jnp.sum(bias_grad * bias_grad))
    factor = jnp.minimum(1.0, CLIP_NORM / norm)
    for i, part in enumerate(parts):
        kernel_step[i * block : (i + 1) * block] = part * factor
    bias_step[...] = bias_grad * factor


def sum_kernel(parts, *rest):
    copies = rest[-1]
    total = jnp.sum(parts[...].astype(F32), 0).astype(copies.dtype)
    copies[...] = jnp.broadcast_to(total[None], copies.shape)


def summed(parts, copies, kind, *after):
    return pl.pallas_call(
        sum_kernel,
        out_shape=jax.ShapeDtypeStruct((copies,) + parts.shape[1:], kind),
        in_specs=vmem(1) + [pl.BlockSpec(memory_space=pl.ANY)] * len(after),
        out_specs=vmem(1)[0],
        compiler_params=pltpu.CompilerParams(vmem_limit_bytes=8 * 2**20),
    )(parts, *after)


def exchanged(copies, axes):
    return lax.all_to_all(copies, axes, 0, 0, tiled=True)


def shape(rows, columns, kind):
    return jax.ShapeDtypeStruct((rows, columns), kind)


def called(kernel, outs, scratch, cost, *args, mebibytes=16):
    return pl.pallas_call(
        kernel,
        out_shape=tuple(outs),
        in_specs=vmem(len(args)),
        out_specs=tuple(vmem(len(outs))),
        scratch_shapes=scratch,
        compiler_params=pltpu.CompilerParams(vmem_limit_bytes=mebibytes * 2**20),
        cost_estimate=pl.CostEstimate(flops=cost, bytes_accessed=2 * cost // 1000, transcendentals=0),
    )(*args)


def per_device(frame, hidden_prev, cell_prev, kernel, bias, grad_hidden, grad_cell):
    inputs, height, breadth = frame.shape
    units = hidden_prev.shape[0]
    channels = inputs + units
    gate_rows = kernel.shape[0]
    flat = (units * height, breadth)
    states = (cell_prev.reshape(flat), grad_hidden.reshape(flat), grad_cell.reshape(flat))

    strip = shape(2 * channels + 3 * units, breadth, F32)
    blocks = (frame.reshape(inputs * height, breadth), hidden_prev.reshape(flat), *states)
    channel_rows = (channels * height, breadth)
    up, down = pl.pallas_call(
        functools.partial(rows_kernel, height=height),
        out_shape=(strip, strip),
        in_specs=[pl.BlockSpec(memory_space=pl.ANY)] * 5,
        out_specs=tuple(vmem(2)),
        scratch_shapes=[pltpu.VMEM(channel_rows, F32)]
        + [pltpu.VMEM(x.shape, x.dtype) for x in blocks]
        + [pltpu.SemaphoreType.DMA((5,))],
        compiler_params=pltpu.CompilerParams(vmem_limit_bytes=60 * 2**20),
        cost_estimate=pl.CostEstimate(flops=1_000_000, bytes_accessed=3_000_000, transcendentals=0),
    )(*blocks)
    edge = shape(channels + 2 * units, LANES, F32)
    columns, weights, joined = called(
        functools.partial(columns_kernel, height=height),
        [edge, shape(gate_rows, 3 * STACK, BF16), shape(*channel_rows, F32)],
        [],
        1_000_000,
        *blocks,
        kernel.T,
    )
    top, bottom = neighbours(up, down, NS)
    (columns,) = called(
        functools.partial(corners_kernel, height=height, units=units), [edge], [], 100_000, columns, top, bottom
    )
    left, right = neighbours(columns, columns, EW)
    bias = bias[:, None]
    field = shape(*flat, F32)
    inner_hidden, inner_cell, inner_back, grads, inner_terms = called(
        forward_kernel,
        [
            field,
            field,
            field,
            shape(gate_rows, (height + 2) * breadth, BF16),
            shape(3 * STACK, gate_rows, F32),
        ],
        [pltpu.VMEM((STACK, (height + 4) * breadth), BF16)],
        1_400_000_000,
        joined,
        top,
        bottom,
        weights,
        bias,
        *states,
    )
    side_grads, side_cells, terms = called(
        functools.partial(sides_kernel, height=height),
        [shape(gate_rows, LANES, BF16), shape(3 * units, LANES, F32), shape(3 * STACK, gate_rows, BF16)],
        [],
        100_000_000,
        columns,
        left,
        right,
        weights,
        bias,
        inner_terms,
    )

    plane = lax.axis_size(PLANE)
    low, high = lax.axis_size("z_lo"), lax.axis_size("z_hi")
    mine = exchanged(terms.reshape(plane, -1, gate_rows), PLANE)
    mine = exchanged(summed(mine, low, F32), "z_lo")
    mine = exchanged(summed(mine, high, F32), "z_hi")
    mine = summed(mine, plane, BF16)
    total = exchanged(mine, PLANE).reshape(3 * STACK, gate_rows)
    hidden, cell, grad_cell_prev, grad_frame, grad_hidden_prev = called(
        backward_kernel,
        [shape(*flat, BF16), field, field, shape(inputs * height, breadth, BF16), shape(*flat, BF16)],
        [pltpu.VMEM((height, 3, channels, breadth), F32), pltpu.VMEM((channels * height, breadth), F32)],
        764_000_000,
        kernel.T,
        grads,
        side_grads,
        side_cells,
        inner_hidden,
        inner_cell,
        inner_back,
    )
    kernel_step, bias_step = called(
        finish_kernel, [shape(9 * channels, gate_rows, F32), shape(1, gate_rows, F32)], [], 1_000_000, total
    )
    whole = (units, height, breadth)
    return (
        hidden.reshape(whole),
        cell.reshape(whole),
        grad_frame.reshape(frame.shape),
        grad_hidden_prev.reshape(whole),
        grad_cell_prev.reshape(whole),
        kernel_step.T,
        bias_step.reshape(gate_rows),
    )


def solution(mesh):
    mesh = Mesh(mesh.devices.reshape(4, 4, 2, 4, 2, 2), EW + NS)
    grid = P(None, NS, EW)
    return jax.shard_map(
        per_device,
        mesh=mesh,
        in_specs=(grid, grid, grid, P(), P(), grid, grid),
        out_specs=(grid, grid, grid, grid, grid, P(), P()),
        check_vma=False,
    )
```

```python
import functools

import jax
import jax.numpy as jnp
from jax import lax
from jax.experimental import pallas as pl
from jax.experimental.pallas import tpu as pltpu
from jax.sharding import Mesh, PartitionSpec as P

CLIP_NORM = 100.0
EW = ("z_hi", "z_lo", "x_hi")
NS = ("y", "x_lo", "core")
PLANE = ("x_hi", "y", "x_lo", "core")
LANES = 128
STACK = 256
BF16 = jnp.bfloat16
F32 = jnp.float32


def vmem(count):
    return [pl.BlockSpec(memory_space=pltpu.VMEM)] * count


def neighbours(to_before, to_after, axes):
    count = lax.axis_size(axes)
    forward = [(i, i + 1) for i in range(count - 1)]
    backward = [(target, source) for source, target in forward]
    return lax.ppermute(to_after, axes, forward), lax.ppermute(to_before, axes, backward)


def sigmoid(x):
    return 0.5 * jnp.tanh(0.5 * x) + 0.5


def rows_kernel(
    frame, hidden_prev, cell_prev, grad_hidden, grad_cell, up, down, joined, frame_here, hidden_here, ends, sems
):
    inputs, height, _ = frame_here.shape
    copies = [
        pltpu.make_async_copy(frame, frame_here, sems.at[0]),
        pltpu.make_async_copy(hidden_prev, hidden_here, sems.at[1]),
    ]
    for i, state in enumerate((cell_prev, grad_hidden, grad_cell)):
        for j, n in enumerate((0, height - 1)):
            copies.append(pltpu.make_async_copy(state.at[:, n, :], ends.at[j, i], sems.at[2 + 2 * i + j]))
    for copy in copies:
        copy.start()
    channels = joined.shape[0] // height
    copies[0].wait()
    joined[: inputs * height] = frame_here[...].astype(F32).reshape(-1, LANES)
    copies[1].wait()
    joined[inputs * height :] = hidden_here[...].astype(F32).reshape(-1, LANES)
    for copy in copies[2:]:
        copy.wait()
    for j, (out, rows) in enumerate(((up, (0, 1)), (down, (height - 2, height - 1)))):
        parts = [joined[pl.ds(n, channels, stride=height), :] for n in rows]
        out[...] = jnp.concatenate(parts + [ends[j, i] for i in range(3)], 0).astype(BF16)


def put_channels(tile, row, place):
    lane = lax.broadcasted_iota(jnp.int32, tile.shape, 1)
    return jnp.where(lane // 4 == place, pltpu.roll(row, (4 * place + 2) % LANES, 1), tile)


def put_state(tile, row, place, slot):
    lane = lax.broadcasted_iota(jnp.int32, tile.shape, 1)
    return jnp.where(lane // 2 == 2 * place + slot // 2, pltpu.roll(row, (4 * place + slot + 1) % LANES, 1), tile)


def columns_kernel(
    frame, hidden_prev, cell_prev, grad_hidden, grad_cell, kernel, columns, weights, joined, *, height
):
    joined[: frame.shape[0]] = frame[...].astype(F32)
    joined[frame.shape[0] :] = hidden_prev[...].astype(F32)
    depth = kernel.shape[0] // 3
    blank = jnp.zeros((STACK - depth, kernel.shape[1]), F32)
    for row_off in range(3):
        part = kernel[...].astype(F32)[row_off * depth : (row_off + 1) * depth]
        weights[:, row_off * STACK : (row_off + 1) * STACK] = jnp.concatenate([part, blank], 0).T.astype(BF16)
    channels = joined.shape[0] // height
    units = cell_prev.shape[0] // height
    tile = jnp.zeros((channels, LANES), F32)
    pairs = jnp.zeros((units, LANES), F32)
    single = jnp.zeros((units, LANES), F32)
    for n in range(height):
        at = pl.ds(n, units, stride=height)
        tile = put_channels(tile, joined[pl.ds(n, channels, stride=height), :], n + 2)
        pairs = put_state(pairs, cell_prev[at, :], n + 1, 0)
        pairs = put_state(pairs, grad_hidden[at, :], n + 1, 2)
        single = put_state(single, grad_cell[at, :], n + 1, 0)
    columns[:channels] = tile
    columns[channels : channels + units] = pairs
    columns[channels + units :] = single


def corners_kernel(columns, top, bottom, out, sent, *, height, units):
    channels = columns.shape[0] - 2 * units
    top = top[...].astype(F32)
    bottom = bottom[...].astype(F32)
    tile = columns[:channels]
    pairs = columns[channels : channels + units]
    single = columns[channels + units :]
    for rows, place, state_place in ((top, 0, 0), (bottom, height + 2, height + 1)):
        for i in range(2):
            tile = put_channels(tile, rows[i * channels : (i + 1) * channels], place + i)
        states = [rows[2 * channels + i * units : 2 * channels + (i + 1) * units] for i in range(3)]
        pairs = put_state(pairs, states[0], state_place, 0)
        pairs = put_state(pairs, states[1], state_place, 2)
        single = put_state(single, states[2], state_place, 0)
    whole = jnp.concatenate([tile, pairs, single], 0)
    out[...] = whole
    spare = jnp.zeros((sent.shape[0] - out.shape[0], LANES), F32)
    sent[...] = jnp.concatenate([whole, spare], 0).astype(BF16)


def gate_step(gates, old, down, grad_cell):
    units = old.shape[0]
    input_gate = sigmoid(gates[:units])
    forget_gate = sigmoid(gates[units : 2 * units])
    cand_gate = jnp.tanh(gates[2 * units : 3 * units])
    output_gate = sigmoid(gates[3 * units :])
    new = forget_gate * old + input_gate * cand_gate
    new_tanh = jnp.tanh(new)
    cell_grad = grad_cell + down * output_gate * (1.0 - new_tanh * new_tanh)
    grads = [
        cell_grad * cand_gate * input_gate * (1.0 - input_gate),
        cell_grad * old * forget_gate * (1.0 - forget_gate),
        cell_grad * input_gate * (1.0 - cand_gate * cand_gate),
        down * new_tanh * output_gate * (1.0 - output_gate),
    ]
    return output_gate * new_tanh, new, cell_grad * forget_gate, jnp.concatenate(grads, 0)


def forward_kernel(
    joined, top, bottom, weights, bias, cell_prev, grad_hidden, grad_cell,
    hidden, cell, grad_cell_prev, grads, terms,
    stacked, hidden_rows, hidden_here, cell_here, back_here, sems,
):
    top = top[...].astype(F32)
    bottom = bottom[...].astype(F32)
    units = bias.shape[0] // 4
    height = cell_prev.shape[0] // units
    channels = joined.shape[0] // height
    spare = STACK - 3 * channels
    ones_row = (lax.broadcasted_iota(jnp.int32, (spare, LANES), 0) == 0).astype(F32)
    for place in range(height + 4):
        if place < 2:
            row = top[place * channels : (place + 1) * channels]
        elif place >= height + 2:
            row = bottom[(place - height - 2) * channels : (place - height - 1) * channels]
        else:
            row = joined[pl.ds(place - 2, channels, stride=height), :]
        stacked[:, place * LANES : (place + 1) * LANES] = jnp.concatenate(
            [pltpu.roll(row, 1, 1), row, pltpu.roll(row, LANES - 1, 1), ones_row], 0
        ).astype(BF16)
    bias_cells = jnp.broadcast_to(bias[...], (4 * units, LANES))
    lane = lax.broadcasted_iota(jnp.int32, (4 * units, LANES), 1)
    middle = (lane > 0) & (lane < LANES - 1)
    for pair in range(height // 2 + 1):
        sums = jnp.zeros((4 * units, 2 * LANES), F32)
        for row_off in range(3):
            start = (2 * pair + row_off) * LANES
            sums = sums + jnp.dot(
                weights[:, row_off * STACK : (row_off + 1) * STACK],
                stacked[:, start : start + 2 * LANES],
                preferred_element_type=F32,
            )
        for half in range(2):
            place = 2 * pair + half
            gates = sums[:, half * LANES : (half + 1) * LANES] + bias_cells
            inside = 0 < place <= height
            if inside:
                at = pl.ds(place - 1, units, stride=height)
                states = [cell_prev[at, :], grad_hidden[at, :], grad_cell[at, :]]
            else:
                rows = bottom if place else top
                states = [rows[2 * channels + i * units : 2 * channels + (i + 1) * units] for i in range(3)]
            new_hidden, new, down, row_grads = gate_step(gates, *states)
            grads[:, place * LANES : (place + 1) * LANES] = jnp.where(middle, row_grads, 0.0).astype(BF16)
            if inside:
                hidden_rows[at, :] = new_hidden
                cell_here[at, :] = new
                back_here[at, :] = down
    hidden_here[...] = hidden_rows[...].astype(BF16)
    copies = [
        pltpu.make_async_copy(source, target, sems.at[i])
        for i, (source, target) in enumerate(
            ((hidden_here, hidden), (cell_here, cell), (back_here, grad_cell_prev))
        )
    ]
    for copy in copies:
        copy.start()
    for row_off in range(3):
        terms[row_off * STACK : (row_off + 1) * STACK] = lax.dot_general(
            stacked[:, (row_off + 1) * LANES : (row_off + 1 + height) * LANES],
            grads[:, LANES : (height + 1) * LANES],
            (((1,), (1,)), ((), ())),
            preferred_element_type=F32,
        )
    for copy in copies:
        copy.wait()


def sides_kernel(columns, left, right, weights, bias, inner_terms, side_grads, side_cells, terms, *, height):
    units = bias.shape[0] // 4
    channels = columns.shape[0] - 2 * units
    spare = STACK - 3 * channels
    left = left[...].astype(F32)
    right = right[...].astype(F32)

    def moved(x, lanes):
        return pltpu.roll(x, lanes % LANES, 1)

    slot = lax.broadcasted_iota(jnp.int32, (channels, LANES), 1) % 4
    own = columns[:channels]
    outer = jnp.where(slot < 2, left[:channels], right[:channels])
    before = jnp.where(
        slot == 0, outer, jnp.where(slot == 1, moved(own, 1), jnp.where(slot == 2, moved(outer, 1), moved(own, 2)))
    )
    at = jnp.where(slot == 0, moved(outer, -1), jnp.where(slot == 3, moved(outer, 1), own))
    after = jnp.where(
        slot == 0, moved(own, -2), jnp.where(slot == 1, moved(outer, -1), jnp.where(slot == 2, moved(own, -1), outer))
    )
    patches = jnp.concatenate([before, at, after], 0)
    ones_row = (lax.broadcasted_iota(jnp.int32, (spare, LANES), 0) == 0).astype(F32)
    stacks = [
        jnp.concatenate([moved(patches, -4 * row_off) if row_off else patches, ones_row], 0).astype(BF16)
        for row_off in range(3)
    ]
    gates = jnp.broadcast_to(bias[...], (4 * units, LANES))
    for row_off in range(3):
        gates = gates + jnp.dot(
            weights[:, row_off * STACK : (row_off + 1) * STACK], stacks[row_off], preferred_element_type=F32
        )
    slot = slot[:units]
    rows = slice(channels, channels + units)
    here, west, east = columns[rows], left[rows], right[rows]
    old = jnp.where(slot == 0, west, jnp.where(slot == 3, moved(east, 2), moved(here, 1)))
    down = jnp.where(slot == 0, moved(west, -2), jnp.where(slot == 3, east, moved(here, -1)))
    rows = slice(channels + units, channels + 2 * units)
    here, west, east = columns[rows], left[rows], right[rows]
    grad_cell = jnp.where(slot == 0, west, jnp.where(slot == 3, moved(east, 2), moved(here, 1)))
    new_hidden, new, back, grads = gate_step(gates, old, down, grad_cell)
    side_cells[:units] = new_hidden
    side_cells[units : 2 * units] = new
    side_cells[2 * units :] = back
    side_grads[...] = grads.astype(BF16)
    lane = lax.broadcasted_iota(jnp.int32, grads.shape, 1)
    inside = (lane >= 4) & (lane < 4 * (height + 1)) & ((lane % 4 == 1) | (lane % 4 == 2))
    grads = jnp.where(inside, grads, 0.0).astype(BF16)
    for row_off in range(3):
        part = slice(row_off * STACK, (row_off + 1) * STACK)
        terms[part] = (
            inner_terms[part]
            + lax.dot_general(
                stacks[row_off], grads, (((1,), (1,)), ((), ())), preferred_element_type=F32
            )
        ).astype(BF16)


def backward_kernel(
    weights, grads, side_grads, side_cells, inner_hidden, inner_cell, inner_back,
    hidden, cell, grad_cell_prev, grad_frame, grad_hidden_prev,
    sums, rows,
):
    height = grads.shape[1] // LANES - 2
    units = hidden.shape[0] // height
    inputs = grad_frame.shape[0] // height
    channels = inputs + units
    lane = lax.broadcasted_iota(jnp.int32, (channels, LANES), 1)
    ends = (lane[:units] == 0) | (lane[:units] == LANES - 1)
    rows[: units * height] = inner_hidden[...].astype(F32)
    for n in range(height):
        at = pl.ds(n, units, stride=height)
        for i, (inner, out) in enumerate(((rows, rows), (inner_cell, cell), (inner_back, grad_cell_prev))):
            side = pltpu.roll(side_cells[i * units : (i + 1) * units], LANES - 4 * (n + 1) - 2, 1)
            out[at, :] = jnp.where(ends, side, inner[at, :])
    hidden[...] = rows[: units * height].astype(BF16)

    outer = jnp.dot(weights[...], side_grads[...], preferred_element_type=F32)
    parts = []
    for col_off in range(3):
        part = jnp.zeros((channels, LANES), F32)
        for row_off in range(3):
            start = (3 * row_off + col_off) * channels
            piece = outer[start : start + channels]
            part = part + (pltpu.roll(piece, LANES - 4 * (2 - row_off), 1) if row_off < 2 else piece)
        parts.append(part)
    slot = lane % 4
    sides = jnp.where((slot == 1) | (slot == 2), parts[1], 0.0) + jnp.where(
        slot == 0,
        pltpu.roll(parts[0], LANES - 1, 1),
        jnp.where(
            slot == 1,
            pltpu.roll(parts[0], LANES - 2, 1),
            jnp.where(slot == 2, pltpu.roll(parts[2], 2, 1), pltpu.roll(parts[2], 1, 1)),
        ),
    )
    for place in range(0, height + 2, 2):
        cells = grads[:, place * LANES : (place + 2) * LANES]
        product = jnp.dot(weights[...], cells, preferred_element_type=F32)
        for half in range(2):
            for row_off in range(3):
                n = place + half + row_off - 2
                if not 0 <= n < height:
                    continue
                for col_off in range(3):
                    start = (3 * row_off + col_off) * channels
                    piece = product[start : start + channels, half * LANES : (half + 1) * LANES]
                    if row_off == 2:
                        sums[n, col_off] = piece
                    else:
                        sums[n, col_off] = sums[n, col_off] + piece
    edge = (lane < 2) | (lane >= LANES - 2)
    for n in range(height):
        total = sums[n, 1] + pltpu.roll(sums[n, 0], LANES - 1, 1) + pltpu.roll(sums[n, 2], 1, 1)
        total = total + jnp.where(edge, pltpu.roll(sides, LANES - 4 * n - 2, 1), 0.0)
        rows[pl.ds(n, channels, stride=height), :] = total
    grad_frame[...] = rows[: inputs * height].astype(BF16)
    grad_hidden_prev[...] = rows[inputs * height :].astype(BF16)


def finish_kernel(total, kernel_step, bias_step):
    block = kernel_step.shape[0] // 3
    parts = [total[i * STACK : i * STACK + block].astype(F32) for i in range(3)]
    bias_grad = total[block : block + 8].astype(F32)[:1]
    norm = jnp.sqrt(sum(jnp.sum(part * part) for part in parts) + jnp.sum(bias_grad * bias_grad))
    factor = jnp.minimum(1.0, CLIP_NORM / norm)
    for i, part in enumerate(parts):
        kernel_step[i * block : (i + 1) * block] = part * factor
    bias_step[...] = bias_grad * factor


def sum_kernel(parts, *rest):
    copies = rest[-1]
    total = jnp.sum(parts[...].astype(F32), 0).astype(copies.dtype)
    copies[...] = jnp.broadcast_to(total[None], copies.shape)


def summed(parts, copies, kind, *after):
    return pl.pallas_call(
        sum_kernel,
        out_shape=jax.ShapeDtypeStruct((copies,) + parts.shape[1:], kind),
        in_specs=vmem(1) + [pl.BlockSpec(memory_space=pl.ANY)] * len(after),
        out_specs=vmem(1)[0],
        compiler_params=pltpu.CompilerParams(vmem_limit_bytes=8 * 2**20),
    )(parts, *after)


def exchanged(copies, axes):
    return lax.all_to_all(copies, axes, 0, 0, tiled=True)


def shape(rows, columns, kind):
    return jax.ShapeDtypeStruct((rows, columns), kind)


def called(kernel, outs, scratch, cost, *args, aliases={}):
    return pl.pallas_call(
        kernel,
        out_shape=tuple(outs),
        in_specs=vmem(len(args)),
        out_specs=tuple(vmem(len(outs))),
        scratch_shapes=scratch,
        input_output_aliases=aliases,
        compiler_params=pltpu.CompilerParams(vmem_limit_bytes=16 * 2**20),
        cost_estimate=pl.CostEstimate(flops=cost, bytes_accessed=2 * cost // 1000, transcendentals=0),
    )(*args)


def per_device(frame, hidden_prev, cell_prev, kernel, bias, grad_hidden, grad_cell):
    inputs, height, breadth = frame.shape
    units = hidden_prev.shape[0]
    channels = inputs + units
    gate_rows = kernel.shape[0]
    flat = (units * height, breadth)
    states = (cell_prev.reshape(flat), grad_hidden.reshape(flat), grad_cell.reshape(flat))

    strip = shape(2 * channels + 3 * units, breadth, BF16)
    blocks = (frame.reshape(inputs * height, breadth), hidden_prev.reshape(flat), *states)
    channel_rows = (channels * height, breadth)
    arrays = (frame, hidden_prev, cell_prev, grad_hidden, grad_cell)
    up, down = pl.pallas_call(
        rows_kernel,
        out_shape=(strip, strip),
        in_specs=[pl.BlockSpec(memory_space=pl.ANY)] * 5,
        out_specs=tuple(vmem(2)),
        scratch_shapes=[
            pltpu.VMEM(channel_rows, F32),
            pltpu.VMEM(frame.shape, BF16),
            pltpu.VMEM(hidden_prev.shape, BF16),
            pltpu.VMEM((2, 3, units, breadth), F32),
            pltpu.SemaphoreType.DMA((8,)),
        ],
        compiler_params=pltpu.CompilerParams(vmem_limit_bytes=60 * 2**20),
        cost_estimate=pl.CostEstimate(flops=1_000_000, bytes_accessed=1_000_000, transcendentals=0),
    )(*arrays)
    edge = shape(channels + 2 * units, LANES, F32)
    columns, weights, joined = called(
        functools.partial(columns_kernel, height=height),
        [edge, shape(gate_rows, 3 * STACK, BF16), shape(*channel_rows, F32)],
        [],
        1_000_000,
        *blocks,
        kernel.T,
    )
    top, bottom = neighbours(up, down, NS)
    sent = shape(-(-(channels + 2 * units) // 16) * 16, LANES, BF16)
    columns, sent = called(
        functools.partial(corners_kernel, height=height, units=units), [edge, sent], [], 100_000, columns, top, bottom
    )
    left, right = neighbours(sent, sent, EW)
    bias = bias[:, None]
    field = shape(*flat, F32)
    inner_hidden, inner_cell, inner_back, grads, inner_terms = pl.pallas_call(
        forward_kernel,
        out_shape=(
            shape(*flat, BF16),
            field,
            field,
            shape(gate_rows, (height + 2) * breadth, BF16),
            shape(3 * STACK, gate_rows, F32),
        ),
        in_specs=vmem(8),
        out_specs=tuple([pl.BlockSpec(memory_space=pl.ANY)] * 3 + vmem(2)),
        scratch_shapes=[pltpu.VMEM((STACK, (height + 4) * breadth), BF16)]
        + [pltpu.VMEM(flat, kind) for kind in (F32, BF16, F32, F32)]
        + [pltpu.SemaphoreType.DMA((3,))],
        compiler_params=pltpu.CompilerParams(vmem_limit_bytes=16 * 2**20),
        cost_estimate=pl.CostEstimate(flops=1_400_000_000, bytes_accessed=4_000_000, transcendentals=700_000),
    )(joined, top, bottom, weights, bias, *states)
    side_grads, side_cells, terms = called(
        functools.partial(sides_kernel, height=height),
        [shape(gate_rows, LANES, BF16), shape(3 * units, LANES, F32), shape(3 * STACK, gate_rows, BF16)],
        [],
        100_000_000,
        columns,
        left,
        right,
        weights,
        bias,
        inner_terms,
    )

    plane = lax.axis_size(PLANE)
    low, high = lax.axis_size("z_lo"), lax.axis_size("z_hi")
    mine = exchanged(terms.reshape(plane, -1, gate_rows), PLANE)
    mine = exchanged(summed(mine, low, F32), "z_lo")
    mine = exchanged(summed(mine, high, F32), "z_hi")
    mine = summed(mine, plane, BF16)
    total = exchanged(mine, PLANE).reshape(3 * STACK, gate_rows)
    hidden, cell, grad_cell_prev, grad_frame, grad_hidden_prev = called(
        backward_kernel,
        [shape(*flat, BF16), field, field, shape(inputs * height, breadth, BF16), shape(*flat, BF16)],
        [pltpu.VMEM((height, 3, channels, breadth), F32), pltpu.VMEM((channels * height, breadth), F32)],
        764_000_000,
        kernel.T,
        grads,
        side_grads,
        side_cells,
        inner_hidden,
        inner_cell,
        inner_back,
        aliases={4: 0, 5: 1, 6: 2},
    )
    kernel_step, bias_step = called(
        finish_kernel, [shape(9 * channels, gate_rows, F32), shape(1, gate_rows, F32)], [], 1_000_000, total
    )
    whole = (units, height, breadth)
    return (
        hidden.reshape(whole),
        cell.reshape(whole),
        grad_frame.reshape(frame.shape),
        grad_hidden_prev.reshape(whole),
        grad_cell_prev.reshape(whole),
        kernel_step.T,
        bias_step.reshape(gate_rows),
    )


def solution(mesh):
    mesh = Mesh(mesh.devices.reshape(4, 4, 2, 4, 2, 2), EW + NS)
    grid = P(None, NS, EW)
    return jax.shard_map(
        per_device,
        mesh=mesh,
        in_specs=(grid, grid, grid, P(), P(), grid, grid),
        out_specs=(grid, grid, grid, grid, grid, P(), P()),
        check_vma=False,
    )
```

```python
import functools

import jax
import jax.numpy as jnp
from jax import lax
from jax.experimental import pallas as pl
from jax.experimental.pallas import tpu as pltpu
from jax.sharding import Mesh, PartitionSpec as P

CLIP_NORM = 100.0
EW = ("z_hi", "z_lo", "x_hi")
NS = ("y", "x_lo", "core")
PLANE = ("x_hi", "y", "x_lo", "core")
LANES = 128
STACK = 256
BF16 = jnp.bfloat16
F32 = jnp.float32


def vmem(count):
    return [pl.BlockSpec(memory_space=pltpu.VMEM)] * count


def swapped(to_pair, to_next, axes):
    count = lax.axis_size(axes)
    pairs = [(i, i ^ 1) for i in range(count) if i ^ 1 < count]
    across = [(i, (i + 1 ^ 1) - 1) for i in range(1, count - 1)]
    other = lax.ppermute(to_next, axes, across)
    return other, lax.ppermute(to_pair, axes, pairs)


def in_order(from_next, from_pair, axis):
    first = lax.axis_index(axis) == 0
    from_pair = from_pair[...].astype(F32)
    from_next = from_next[...].astype(F32)
    return jnp.where(first, from_next, from_pair), jnp.where(first, from_pair, from_next)


def sigmoid(x):
    return 0.5 * jnp.tanh(0.5 * x) + 0.5


def rows_kernel(
    frame, hidden_prev, cell_prev, grad_hidden, grad_cell, to_pair, to_next, joined, frame_here, hidden_here, ends, sems
):
    inputs, height, _ = frame_here.shape
    copies = [
        pltpu.make_async_copy(frame, frame_here, sems.at[0]),
        pltpu.make_async_copy(hidden_prev, hidden_here, sems.at[1]),
    ]
    for i, state in enumerate((cell_prev, grad_hidden, grad_cell)):
        for j, n in enumerate((0, height - 1)):
            copies.append(pltpu.make_async_copy(state.at[:, n, :], ends.at[j, i], sems.at[2 + 2 * i + j]))
    for copy in copies:
        copy.start()
    channels = joined.shape[0] // height
    copies[0].wait()
    joined[: inputs * height] = frame_here[...].astype(F32).reshape(-1, LANES)
    copies[1].wait()
    joined[inputs * height :] = hidden_here[...].astype(F32).reshape(-1, LANES)
    for copy in copies[2:]:
        copy.wait()
    strips = []
    for j, rows in enumerate(((0, 1), (height - 2, height - 1))):
        parts = [joined[pl.ds(n, channels, stride=height), :] for n in rows]
        strips.append(jnp.concatenate(parts + [ends[j, i] for i in range(3)], 0))
    first = lax.axis_index(NS[-1]) == 0
    to_pair[...] = jnp.where(first, strips[1], strips[0]).astype(BF16)
    to_next[...] = jnp.where(first, strips[0], strips[1]).astype(BF16)


def put_channels(tile, row, place):
    lane = lax.broadcasted_iota(jnp.int32, tile.shape, 1)
    return jnp.where(lane // 4 == place, pltpu.roll(row, (4 * place + 2) % LANES, 1), tile)


def put_state(tile, row, place, slot):
    lane = lax.broadcasted_iota(jnp.int32, tile.shape, 1)
    return jnp.where(lane // 2 == 2 * place + slot // 2, pltpu.roll(row, (4 * place + slot + 1) % LANES, 1), tile)


def stack_of(row):
    spare = STACK - 3 * row.shape[0]
    ones_row = (lax.broadcasted_iota(jnp.int32, (spare, LANES), 0) == 0).astype(F32)
    return jnp.concatenate([pltpu.roll(row, 1, 1), row, pltpu.roll(row, LANES - 1, 1), ones_row], 0).astype(BF16)


def columns_kernel(
    frame, hidden_prev, cell_prev, grad_hidden, grad_cell, kernel, columns, weights, stacked, joined, *, height
):
    joined[: frame.shape[0]] = frame[...].astype(F32)
    joined[frame.shape[0] :] = hidden_prev[...].astype(F32)
    depth = kernel.shape[0] // 3
    blank = jnp.zeros((STACK - depth, kernel.shape[1]), F32)
    for row_off in range(3):
        part = kernel[...].astype(F32)[row_off * depth : (row_off + 1) * depth]
        weights[:, row_off * STACK : (row_off + 1) * STACK] = jnp.concatenate([part, blank], 0).T.astype(BF16)
    channels = joined.shape[0] // height
    units = cell_prev.shape[0] // height
    tile = jnp.zeros((channels, LANES), F32)
    pairs = jnp.zeros((units, LANES), F32)
    single = jnp.zeros((units, LANES), F32)
    for n in range(height):
        at = pl.ds(n, units, stride=height)
        row = joined[pl.ds(n, channels, stride=height), :]
        stacked[:, n * LANES : (n + 1) * LANES] = stack_of(row)
        tile = put_channels(tile, row, n + 2)
        pairs = put_state(pairs, cell_prev[at, :], n + 1, 0)
        pairs = put_state(pairs, grad_hidden[at, :], n + 1, 2)
        single = put_state(single, grad_cell[at, :], n + 1, 0)
    columns[:channels] = tile
    columns[channels : channels + units] = pairs
    columns[channels + units :] = single


def corners_kernel(columns, from_next, from_pair, out, sent, *, height, units):
    channels = columns.shape[0] - 2 * units
    top, bottom = in_order(from_next, from_pair, NS[-1])
    tile = columns[:channels]
    pairs = columns[channels : channels + units]
    single = columns[channels + units :]
    for rows, place, state_place in ((top, 0, 0), (bottom, height + 2, height + 1)):
        for i in range(2):
            tile = put_channels(tile, rows[i * channels : (i + 1) * channels], place + i)
        states = [rows[2 * channels + i * units : 2 * channels + (i + 1) * units] for i in range(3)]
        pairs = put_state(pairs, states[0], state_place, 0)
        pairs = put_state(pairs, states[1], state_place, 2)
        single = put_state(single, states[2], state_place, 0)
    whole = jnp.concatenate([tile, pairs, single], 0)
    out[...] = whole
    spare = jnp.zeros((sent.shape[0] - out.shape[0], LANES), F32)
    sent[...] = jnp.concatenate([whole, spare], 0).astype(BF16)


def gate_step(gates, old, down, grad_cell):
    units = old.shape[0]
    input_gate = sigmoid(gates[:units])
    forget_gate = sigmoid(gates[units : 2 * units])
    cand_gate = jnp.tanh(gates[2 * units : 3 * units])
    output_gate = sigmoid(gates[3 * units :])
    new = forget_gate * old + input_gate * cand_gate
    new_tanh = jnp.tanh(new)
    cell_grad = grad_cell + down * output_gate * (1.0 - new_tanh * new_tanh)
    grads = [
        cell_grad * cand_gate * input_gate * (1.0 - input_gate),
        cell_grad * old * forget_gate * (1.0 - forget_gate),
        cell_grad * input_gate * (1.0 - cand_gate * cand_gate),
        down * new_tanh * output_gate * (1.0 - output_gate),
    ]
    return output_gate * new_tanh, new, cell_grad * forget_gate, jnp.concatenate(grads, 0)


def forward_kernel(
    stacked, from_next, from_pair, weights, bias, cell_prev, grad_hidden, grad_cell,
    hidden, cell, grad_cell_prev, grads, terms,
    hidden_rows, hidden_here, cell_here, back_here, sems,
):
    units = bias.shape[0] // 4
    height = cell_prev.shape[0] // units
    channels = (from_pair.shape[0] - 3 * units) // 2
    top, bottom = in_order(from_next, from_pair, NS[-1])
    north = [stack_of(top[i * channels : (i + 1) * channels]) for i in range(2)]
    south = [stack_of(bottom[i * channels : (i + 1) * channels]) for i in range(2)]

    def two_rows(place):
        if 2 <= place <= height:
            return stacked[:, (place - 2) * LANES : place * LANES]
        outer = [None] * (height + 4)
        outer[:2], outer[-2:] = north, south
        outer[2], outer[-3] = stacked[:, :LANES], stacked[:, (height - 1) * LANES :]
        return jnp.concatenate(outer[place : place + 2], 1)

    def copy_out(half):
        rows = pl.ds(half * (height // 2), height // 2)
        return [
            pltpu.make_async_copy(here.at[:, rows, :], out.at[:, rows, :], sems.at[2 * half + i])
            for i, (here, out) in enumerate(((cell_here, cell), (back_here, grad_cell_prev)))
        ]

    cell_rows = cell_here.reshape(units * height, LANES)
    back_rows = back_here.reshape(units * height, LANES)
    bias_cells = jnp.broadcast_to(bias[...], (4 * units, LANES))
    lane = lax.broadcasted_iota(jnp.int32, (4 * units, LANES), 1)
    middle = (lane > 0) & (lane < LANES - 1)
    for pair in range(height // 2 + 1):
        sums = jnp.zeros((4 * units, 2 * LANES), F32)
        for row_off in range(3):
            sums = sums + jnp.dot(
                weights[:, row_off * STACK : (row_off + 1) * STACK],
                two_rows(2 * pair + row_off),
                preferred_element_type=F32,
            )
        for half in range(2):
            place = 2 * pair + half
            gates = sums[:, half * LANES : (half + 1) * LANES] + bias_cells
            inside = 0 < place <= height
            if inside:
                at = pl.ds(place - 1, units, stride=height)
                states = [cell_prev[at, :], grad_hidden[at, :], grad_cell[at, :]]
            else:
                rows = bottom if place else top
                states = [rows[2 * channels + i * units : 2 * channels + (i + 1) * units] for i in range(3)]
            new_hidden, new, down, row_grads = gate_step(gates, *states)
            grads[:, place * LANES : (place + 1) * LANES] = jnp.where(middle, row_grads, 0.0).astype(BF16)
            if inside:
                hidden_rows[at, :] = new_hidden
                cell_rows[at, :] = new
                back_rows[at, :] = down
        if pair == height // 4:
            for copy in copy_out(0):
                copy.start()
    hidden_here[...] = hidden_rows[...].astype(BF16)
    hidden_copy = pltpu.make_async_copy(hidden_here, hidden, sems.at[4])
    copies = copy_out(0) + copy_out(1) + [hidden_copy]
    for copy in copies[2:]:
        copy.start()
    own = grads[:, LANES : (height + 1) * LANES]
    for row_off in range(3):
        if row_off == 0:
            rows = jnp.concatenate([north[1], stacked[:, : (height - 1) * LANES]], 1)
        elif row_off == 1:
            rows = stacked[...]
        else:
            rows = jnp.concatenate([stacked[:, LANES:], south[0]], 1)
        terms[row_off * STACK : (row_off + 1) * STACK] = lax.dot_general(
            rows, own, (((1,), (1,)), ((), ())), preferred_element_type=F32
        )
    for copy in copies:
        copy.wait()


def sides_kernel(
    columns, from_next, from_pair, weights, bias, inner_terms, side_grads, side_cells, terms, *, height
):
    units = bias.shape[0] // 4
    channels = columns.shape[0] - 2 * units
    spare = STACK - 3 * channels
    left, right = in_order(from_next, from_pair, EW[-1])

    def moved(x, lanes):
        return pltpu.roll(x, lanes % LANES, 1)

    slot = lax.broadcasted_iota(jnp.int32, (channels, LANES), 1) % 4
    own = columns[:channels]
    outer = jnp.where(slot < 2, left[:channels], right[:channels])
    before = jnp.where(
        slot == 0, outer, jnp.where(slot == 1, moved(own, 1), jnp.where(slot == 2, moved(outer, 1), moved(own, 2)))
    )
    at = jnp.where(slot == 0, moved(outer, -1), jnp.where(slot == 3, moved(outer, 1), own))
    after = jnp.where(
        slot == 0, moved(own, -2), jnp.where(slot == 1, moved(outer, -1), jnp.where(slot == 2, moved(own, -1), outer))
    )
    patches = jnp.concatenate([before, at, after], 0)
    ones_row = (lax.broadcasted_iota(jnp.int32, (spare, LANES), 0) == 0).astype(F32)
    stacks = [
        jnp.concatenate([moved(patches, -4 * row_off) if row_off else patches, ones_row], 0).astype(BF16)
        for row_off in range(3)
    ]
    gates = jnp.broadcast_to(bias[...], (4 * units, LANES))
    for row_off in range(3):
        gates = gates + jnp.dot(
            weights[:, row_off * STACK : (row_off + 1) * STACK], stacks[row_off], preferred_element_type=F32
        )
    slot = slot[:units]
    rows = slice(channels, channels + units)
    here, west, east = columns[rows], left[rows], right[rows]
    old = jnp.where(slot == 0, west, jnp.where(slot == 3, moved(east, 2), moved(here, 1)))
    down = jnp.where(slot == 0, moved(west, -2), jnp.where(slot == 3, east, moved(here, -1)))
    rows = slice(channels + units, channels + 2 * units)
    here, west, east = columns[rows], left[rows], right[rows]
    grad_cell = jnp.where(slot == 0, west, jnp.where(slot == 3, moved(east, 2), moved(here, 1)))
    new_hidden, new, back, grads = gate_step(gates, old, down, grad_cell)
    side_cells[:units] = new_hidden
    side_cells[units : 2 * units] = new
    side_cells[2 * units :] = back
    side_grads[...] = grads.astype(BF16)
    lane = lax.broadcasted_iota(jnp.int32, grads.shape, 1)
    inside = (lane >= 4) & (lane < 4 * (height + 1)) & ((lane % 4 == 1) | (lane % 4 == 2))
    grads = jnp.where(inside, grads, 0.0).astype(BF16)
    for row_off in range(3):
        part = slice(row_off * STACK, (row_off + 1) * STACK)
        terms[part] = (
            inner_terms[part]
            + lax.dot_general(
                stacks[row_off], grads, (((1,), (1,)), ((), ())), preferred_element_type=F32
            )
        ).astype(BF16)


def backward_kernel(
    weights, grads, side_grads, side_cells, inner_hidden, inner_cell, inner_back,
    hidden, cell, grad_cell_prev, grad_frame, grad_hidden_prev,
    sums, rows,
):
    height = grads.shape[1] // LANES - 2
    units = hidden.shape[0] // height
    inputs = grad_frame.shape[0] // height
    channels = inputs + units
    lane = lax.broadcasted_iota(jnp.int32, (channels, LANES), 1)
    ends = (lane[:units] == 0) | (lane[:units] == LANES - 1)
    rows[: units * height] = inner_hidden[...].astype(F32)
    for n in range(height):
        at = pl.ds(n, units, stride=height)
        for i, (inner, out) in enumerate(((rows, rows), (inner_cell, cell), (inner_back, grad_cell_prev))):
            side = pltpu.roll(side_cells[i * units : (i + 1) * units], LANES - 4 * (n + 1) - 2, 1)
            out[at, :] = jnp.where(ends, side, inner[at, :])
    hidden[...] = rows[: units * height].astype(BF16)

    outer = jnp.dot(weights[...], side_grads[...], preferred_element_type=F32)
    parts = []
    for col_off in range(3):
        part = jnp.zeros((channels, LANES), F32)
        for row_off in range(3):
            start = (3 * row_off + col_off) * channels
            piece = outer[start : start + channels]
            part = part + (pltpu.roll(piece, LANES - 4 * (2 - row_off), 1) if row_off < 2 else piece)
        parts.append(part)
    slot = lane % 4
    sides = jnp.where((slot == 1) | (slot == 2), parts[1], 0.0) + jnp.where(
        slot == 0,
        pltpu.roll(parts[0], LANES - 1, 1),
        jnp.where(
            slot == 1,
            pltpu.roll(parts[0], LANES - 2, 1),
            jnp.where(slot == 2, pltpu.roll(parts[2], 2, 1), pltpu.roll(parts[2], 1, 1)),
        ),
    )
    for place in range(0, height + 2, 2):
        cells = grads[:, place * LANES : (place + 2) * LANES]
        product = jnp.dot(weights[...], cells, preferred_element_type=F32)
        for half in range(2):
            for row_off in range(3):
                n = place + half + row_off - 2
                if not 0 <= n < height:
                    continue
                for col_off in range(3):
                    start = (3 * row_off + col_off) * channels
                    piece = product[start : start + channels, half * LANES : (half + 1) * LANES]
                    if row_off == 2:
                        sums[n, col_off] = piece
                    else:
                        sums[n, col_off] = sums[n, col_off] + piece
    edge = (lane < 2) | (lane >= LANES - 2)
    for n in range(height):
        total = sums[n, 1] + pltpu.roll(sums[n, 0], LANES - 1, 1) + pltpu.roll(sums[n, 2], 1, 1)
        total = total + jnp.where(edge, pltpu.roll(sides, LANES - 4 * n - 2, 1), 0.0)
        rows[pl.ds(n, channels, stride=height), :] = total
    grad_frame[...] = rows[: inputs * height].astype(BF16)
    grad_hidden_prev[...] = rows[inputs * height :].astype(BF16)


def finish_kernel(total, kernel_step, bias_step):
    block = kernel_step.shape[0] // 3
    parts = [total[i * STACK : i * STACK + block].astype(F32) for i in range(3)]
    bias_grad = total[block : block + 8].astype(F32)[:1]
    norm = jnp.sqrt(sum(jnp.sum(part * part) for part in parts) + jnp.sum(bias_grad * bias_grad))
    factor = jnp.minimum(1.0, CLIP_NORM / norm)
    for i, part in enumerate(parts):
        kernel_step[i * block : (i + 1) * block] = part * factor
    bias_step[...] = bias_grad * factor


def sum_kernel(parts, *rest):
    copies = rest[-1]
    total = jnp.sum(parts[...].astype(F32), 0).astype(copies.dtype)
    copies[...] = jnp.broadcast_to(total[None], copies.shape)


def summed(parts, copies, kind, *after):
    return pl.pallas_call(
        sum_kernel,
        out_shape=jax.ShapeDtypeStruct((copies,) + parts.shape[1:], kind),
        in_specs=vmem(1) + [pl.BlockSpec(memory_space=pl.ANY)] * len(after),
        out_specs=vmem(1)[0],
        compiler_params=pltpu.CompilerParams(vmem_limit_bytes=8 * 2**20),
    )(parts, *after)


def exchanged(copies, axes):
    return lax.all_to_all(copies, axes, 0, 0, tiled=True)


def shape(rows, columns, kind):
    return jax.ShapeDtypeStruct((rows, columns), kind)


def called(kernel, outs, scratch, cost, *args, aliases={}):
    return pl.pallas_call(
        kernel,
        out_shape=tuple(outs),
        in_specs=vmem(len(args)),
        out_specs=tuple(vmem(len(outs))),
        scratch_shapes=scratch,
        input_output_aliases=aliases,
        compiler_params=pltpu.CompilerParams(vmem_limit_bytes=16 * 2**20),
        cost_estimate=pl.CostEstimate(flops=cost, bytes_accessed=2 * cost // 1000, transcendentals=0),
    )(*args)


def per_device(frame, hidden_prev, cell_prev, kernel, bias, grad_hidden, grad_cell):
    inputs, height, breadth = frame.shape
    units = hidden_prev.shape[0]
    channels = inputs + units
    gate_rows = kernel.shape[0]
    flat = (units * height, breadth)
    states = (cell_prev.reshape(flat), grad_hidden.reshape(flat), grad_cell.reshape(flat))

    strip = shape(2 * channels + 3 * units, breadth, BF16)
    blocks = (frame.reshape(inputs * height, breadth), hidden_prev.reshape(flat), *states)
    channel_rows = (channels * height, breadth)
    arrays = (frame, hidden_prev, cell_prev, grad_hidden, grad_cell)
    to_pair, to_next = pl.pallas_call(
        rows_kernel,
        out_shape=(strip, strip),
        in_specs=[pl.BlockSpec(memory_space=pl.ANY)] * 5,
        out_specs=tuple(vmem(2)),
        scratch_shapes=[
            pltpu.VMEM(channel_rows, F32),
            pltpu.VMEM(frame.shape, BF16),
            pltpu.VMEM(hidden_prev.shape, BF16),
            pltpu.VMEM((2, 3, units, breadth), F32),
            pltpu.SemaphoreType.DMA((8,)),
        ],
        compiler_params=pltpu.CompilerParams(vmem_limit_bytes=60 * 2**20),
        cost_estimate=pl.CostEstimate(flops=1_000_000, bytes_accessed=1_000_000, transcendentals=0),
    )(*arrays)
    edge = shape(channels + 2 * units, LANES, F32)
    columns, weights, stacked = called(
        functools.partial(columns_kernel, height=height),
        [edge, shape(gate_rows, 3 * STACK, BF16), shape(STACK, height * breadth, BF16)],
        [pltpu.VMEM(channel_rows, F32)],
        1_000_000,
        *blocks,
        kernel.T,
    )
    rows = swapped(to_pair, to_next, NS)
    sent = shape(-(-(channels + 2 * units) // 16) * 16, LANES, BF16)
    columns, sent = called(
        functools.partial(corners_kernel, height=height, units=units), [edge, sent], [], 100_000, columns, *rows
    )
    sides = swapped(sent, sent, EW)
    bias = bias[:, None]
    field = shape(*flat, F32)
    cube = jax.ShapeDtypeStruct((units, height, breadth), F32)
    inner_hidden, inner_cell, inner_back, grads, inner_terms = pl.pallas_call(
        forward_kernel,
        out_shape=(
            shape(*flat, BF16),
            cube,
            cube,
            shape(gate_rows, (height + 2) * breadth, BF16),
            shape(3 * STACK, gate_rows, F32),
        ),
        in_specs=vmem(8),
        out_specs=tuple([pl.BlockSpec(memory_space=pl.ANY)] * 3 + vmem(2)),
        scratch_shapes=[
            pltpu.VMEM(flat, F32),
            pltpu.VMEM(flat, BF16),
            pltpu.VMEM(cube.shape, F32),
            pltpu.VMEM(cube.shape, F32),
            pltpu.SemaphoreType.DMA((5,)),
        ],
        compiler_params=pltpu.CompilerParams(vmem_limit_bytes=16 * 2**20),
        cost_estimate=pl.CostEstimate(flops=1_400_000_000, bytes_accessed=4_000_000, transcendentals=700_000),
    )(stacked, *rows, weights, bias, *states)
    side_grads, side_cells, terms = called(
        functools.partial(sides_kernel, height=height),
        [shape(gate_rows, LANES, BF16), shape(3 * units, LANES, F32), shape(3 * STACK, gate_rows, BF16)],
        [],
        100_000_000,
        columns,
        *sides,
        weights,
        bias,
        inner_terms,
    )

    plane = lax.axis_size(PLANE)
    low, high = lax.axis_size("z_lo"), lax.axis_size("z_hi")
    mine = exchanged(terms.reshape(plane, -1, gate_rows), PLANE)
    mine = exchanged(summed(mine, low, F32), "z_lo")
    mine = exchanged(summed(mine, high, F32), "z_hi")
    mine = summed(mine, plane, BF16)
    total = exchanged(mine, PLANE).reshape(3 * STACK, gate_rows)
    hidden, cell, grad_cell_prev, grad_frame, grad_hidden_prev = called(
        backward_kernel,
        [shape(*flat, BF16), field, field, shape(inputs * height, breadth, BF16), shape(*flat, BF16)],
        [pltpu.VMEM((height, 3, channels, breadth), F32), pltpu.VMEM((channels * height, breadth), F32)],
        764_000_000,
        kernel.T,
        grads,
        side_grads,
        side_cells,
        inner_hidden,
        inner_cell.reshape(flat),
        inner_back.reshape(flat),
        aliases={4: 0, 5: 1, 6: 2},
    )
    kernel_step, bias_step = called(
        finish_kernel, [shape(9 * channels, gate_rows, F32), shape(1, gate_rows, F32)], [], 1_000_000, total
    )
    whole = (units, height, breadth)
    return (
        hidden.reshape(whole),
        cell.reshape(whole),
        grad_frame.reshape(frame.shape),
        grad_hidden_prev.reshape(whole),
        grad_cell_prev.reshape(whole),
        kernel_step.T,
        bias_step.reshape(gate_rows),
    )


def solution(mesh):
    mesh = Mesh(mesh.devices.reshape(4, 4, 2, 4, 2, 2), EW + NS)
    grid = P(None, NS, EW)
    return jax.shard_map(
        per_device,
        mesh=mesh,
        in_specs=(grid, grid, grid, P(), P(), grid, grid),
        out_specs=(grid, grid, grid, grid, grid, P(), P()),
        check_vma=False,
    )
```

```python
import functools

import jax
import jax.numpy as jnp
from jax import lax
from jax.experimental import pallas as pl
from jax.experimental.pallas import tpu as pltpu
from jax.sharding import Mesh, PartitionSpec as P

CLIP_NORM = 100.0
EW = ("z_hi", "z_lo", "x_hi")
NS = ("y", "x_lo", "core")
PLANE = ("x_hi", "y", "x_lo", "core")
LANES = 128
STACK = 256
STEP = 6
BF16 = jnp.bfloat16
F32 = jnp.float32


def vmem(count):
    return [pl.BlockSpec(memory_space=pltpu.VMEM)] * count


def swapped(to_pair, to_next, axes):
    count = lax.axis_size(axes)
    pairs = [(i, i ^ 1) for i in range(count) if i ^ 1 < count]
    across = [(i, (i + 1 ^ 1) - 1) for i in range(1, count - 1)]
    other = lax.ppermute(to_next, axes, across)
    return other, lax.ppermute(to_pair, axes, pairs)


def in_order(from_next, from_pair, axis):
    first = lax.axis_index(axis) == 0
    from_pair = from_pair[...].astype(F32)
    from_next = from_next[...].astype(F32)
    return jnp.where(first, from_next, from_pair), jnp.where(first, from_pair, from_next)


def sigmoid(x):
    return 0.5 * jnp.tanh(0.5 * x) + 0.5


def rows_kernel(
    frame, hidden_prev, cell_prev, grad_hidden, grad_cell, to_pair, to_next, joined, frame_here, hidden_here, ends, sems
):
    inputs, height, _ = frame_here.shape
    copies = [
        pltpu.make_async_copy(frame, frame_here, sems.at[0]),
        pltpu.make_async_copy(hidden_prev, hidden_here, sems.at[1]),
    ]
    for i, state in enumerate((cell_prev, grad_hidden, grad_cell)):
        for j, n in enumerate((0, height - 1)):
            copies.append(pltpu.make_async_copy(state.at[:, n, :], ends.at[j, i], sems.at[2 + 2 * i + j]))
    for copy in copies:
        copy.start()
    channels = joined.shape[0] // height
    copies[0].wait()
    joined[: inputs * height] = frame_here[...].astype(F32).reshape(-1, LANES)
    copies[1].wait()
    joined[inputs * height :] = hidden_here[...].astype(F32).reshape(-1, LANES)
    for copy in copies[2:]:
        copy.wait()
    strips = []
    for j, rows in enumerate(((0, 1), (height - 2, height - 1))):
        parts = [joined[pl.ds(n, channels, stride=height), :] for n in rows]
        strips.append(jnp.concatenate(parts + [ends[j, i] for i in range(3)], 0))
    first = lax.axis_index(NS[-1]) == 0
    to_pair[...] = jnp.where(first, strips[1], strips[0]).astype(BF16)
    to_next[...] = jnp.where(first, strips[0], strips[1]).astype(BF16)


def put_channels(tile, row, place):
    lane = lax.broadcasted_iota(jnp.int32, tile.shape, 1)
    return jnp.where(lane // STEP == place, pltpu.roll(row, (STEP * place + 2) % LANES, 1), tile)


def put_state(tile, row, place, slot):
    lane = lax.broadcasted_iota(jnp.int32, tile.shape, 1)
    start = STEP * place + slot
    return jnp.where(lane // 2 == start // 2, pltpu.roll(row, (start + 1) % LANES, 1), tile)


def stack_of(row):
    spare = STACK - 3 * row.shape[0]
    ones_row = (lax.broadcasted_iota(jnp.int32, (spare, LANES), 0) == 0).astype(F32)
    return jnp.concatenate([pltpu.roll(row, 1, 1), row, pltpu.roll(row, LANES - 1, 1), ones_row], 0).astype(BF16)


def columns_kernel(frame, hidden_prev, cell_prev, grad_hidden, grad_cell, columns, stacked, joined, *, height):
    joined[: frame.shape[0]] = frame[...].astype(F32)
    joined[frame.shape[0] :] = hidden_prev[...].astype(F32)
    channels = joined.shape[0] // height
    units = cell_prev.shape[0] // height
    tile = jnp.zeros((channels, LANES), F32)
    states = jnp.zeros((units, LANES), F32)
    for n in range(height):
        at = pl.ds(n, units, stride=height)
        row = joined[pl.ds(n, channels, stride=height), :]
        stacked[:, n * LANES : (n + 1) * LANES] = stack_of(row)
        tile = put_channels(tile, row, n + 2)
        for i, state in enumerate((cell_prev, grad_hidden, grad_cell)):
            states = put_state(states, state[at, :], n + 1, 2 * i)
    columns[:channels] = tile
    columns[channels:] = states


def moved(x, lanes):
    return pltpu.roll(x, lanes % LANES, 1) if lanes else x


def by_slot(slot, *choices):
    out = choices[-1]
    for i in range(len(choices) - 2, -1, -1):
        out = jnp.where(slot == i, choices[i], out)
    return out


def corners_kernel(columns, from_next, from_pair, out, to_next, to_pair, *, height, units):
    channels = columns.shape[0] - units
    top, bottom = in_order(from_next, from_pair, NS[-1])
    tile = columns[:channels]
    states = columns[channels:]
    for rows, place, state_place in ((top, 0, 0), (bottom, height + 2, height + 1)):
        for i in range(2):
            tile = put_channels(tile, rows[i * channels : (i + 1) * channels], place + i)
        for i in range(3):
            start = 2 * channels + i * units
            states = put_state(states, rows[start : start + units], state_place, 2 * i)
    out[:channels] = tile
    out[channels:] = states
    slot = lax.broadcasted_iota(jnp.int32, (channels, LANES), 1) % STEP
    blank = jnp.zeros((channels - units, LANES), F32)
    east = [jnp.concatenate([moved(states, k), blank], 0) for k in (2, 1, 0)]
    west = [jnp.concatenate([moved(states, k), blank], 0) for k in (1, 0, -1)]
    east = by_slot(slot, tile, tile, *east)
    west = by_slot(slot, moved(tile, -2), moved(tile, -2), *west)
    spare = jnp.zeros((to_pair.shape[0] - channels, LANES), F32)
    first = lax.axis_index(EW[-1]) == 0
    to_pair[...] = jnp.concatenate([jnp.where(first, east, west), spare], 0).astype(BF16)
    to_next[...] = jnp.concatenate([jnp.where(first, west, east), spare], 0).astype(BF16)


def gate_step(gates, old, down, grad_cell):
    units = old.shape[0]
    input_gate = sigmoid(gates[:units])
    forget_gate = sigmoid(gates[units : 2 * units])
    cand_gate = jnp.tanh(gates[2 * units : 3 * units])
    output_gate = sigmoid(gates[3 * units :])
    new = forget_gate * old + input_gate * cand_gate
    new_tanh = jnp.tanh(new)
    cell_grad = grad_cell + down * output_gate * (1.0 - new_tanh * new_tanh)
    grads = [
        cell_grad * cand_gate * input_gate * (1.0 - input_gate),
        cell_grad * old * forget_gate * (1.0 - forget_gate),
        cell_grad * input_gate * (1.0 - cand_gate * cand_gate),
        down * new_tanh * output_gate * (1.0 - output_gate),
    ]
    return output_gate * new_tanh, new, cell_grad * forget_gate, jnp.concatenate(grads, 0)


def forward_kernel(
    stacked, from_next, from_pair, kernel, bias, cell_prev, grad_hidden, grad_cell,
    hidden, cell, grad_cell_prev, grads, terms, weights,
    hidden_rows, hidden_here, cell_here, back_here, sems,
):
    depth = kernel.shape[0] // 3
    blank = jnp.zeros((STACK - depth, kernel.shape[1]), F32)
    for row_off in range(3):
        part = kernel[...].astype(F32)[row_off * depth : (row_off + 1) * depth]
        weights[:, row_off * STACK : (row_off + 1) * STACK] = jnp.concatenate([part, blank], 0).T.astype(BF16)
    units = bias.shape[0] // 4
    height = cell_prev.shape[0] // units
    channels = (from_pair.shape[0] - 3 * units) // 2
    top, bottom = in_order(from_next, from_pair, NS[-1])
    north = [stack_of(top[i * channels : (i + 1) * channels]) for i in range(2)]
    south = [stack_of(bottom[i * channels : (i + 1) * channels]) for i in range(2)]

    def two_rows(place):
        if 2 <= place <= height:
            return stacked[:, (place - 2) * LANES : place * LANES]
        outer = [None] * (height + 4)
        outer[:2], outer[-2:] = north, south
        outer[2], outer[-3] = stacked[:, :LANES], stacked[:, (height - 1) * LANES :]
        return jnp.concatenate(outer[place : place + 2], 1)

    def copy_out(half):
        rows = pl.ds(half * (height // 2), height // 2)
        return [
            pltpu.make_async_copy(here.at[:, rows, :], out.at[:, rows, :], sems.at[2 * half + i])
            for i, (here, out) in enumerate(((cell_here, cell), (back_here, grad_cell_prev)))
        ]

    cell_rows = cell_here.reshape(units * height, LANES)
    back_rows = back_here.reshape(units * height, LANES)
    bias_cells = jnp.broadcast_to(bias[...], (4 * units, LANES))
    lane = lax.broadcasted_iota(jnp.int32, (4 * units, LANES), 1)
    middle = (lane > 0) & (lane < LANES - 1)
    for pair in range(height // 2 + 1):
        sums = jnp.zeros((4 * units, 2 * LANES), F32)
        for row_off in range(3):
            sums = sums + jnp.dot(
                weights[:, row_off * STACK : (row_off + 1) * STACK],
                two_rows(2 * pair + row_off),
                preferred_element_type=F32,
            )
        for half in range(2):
            place = 2 * pair + half
            gates = sums[:, half * LANES : (half + 1) * LANES] + bias_cells
            inside = 0 < place <= height
            if inside:
                at = pl.ds(place - 1, units, stride=height)
                states = [cell_prev[at, :], grad_hidden[at, :], grad_cell[at, :]]
            else:
                rows = bottom if place else top
                states = [rows[2 * channels + i * units : 2 * channels + (i + 1) * units] for i in range(3)]
            new_hidden, new, down, row_grads = gate_step(gates, *states)
            grads[:, place * LANES : (place + 1) * LANES] = jnp.where(middle, row_grads, 0.0).astype(BF16)
            if inside:
                hidden_rows[at, :] = new_hidden
                cell_rows[at, :] = new
                back_rows[at, :] = down
        if pair == height // 4:
            for copy in copy_out(0):
                copy.start()
    hidden_here[...] = hidden_rows[...].astype(BF16)
    hidden_copy = pltpu.make_async_copy(hidden_here, hidden, sems.at[4])
    copies = copy_out(0) + copy_out(1) + [hidden_copy]
    for copy in copies[2:]:
        copy.start()
    own = grads[:, LANES : (height + 1) * LANES]
    for row_off in range(3):
        if row_off == 0:
            rows = jnp.concatenate([north[1], stacked[:, : (height - 1) * LANES]], 1)
        elif row_off == 1:
            rows = stacked[...]
        else:
            rows = jnp.concatenate([stacked[:, LANES:], south[0]], 1)
        terms[row_off * STACK : (row_off + 1) * STACK] = lax.dot_general(
            rows, own, (((1,), (1,)), ((), ())), preferred_element_type=F32
        )
    for copy in copies:
        copy.wait()


def sides_kernel(
    columns, from_next, from_pair, weights, bias, inner_terms, side_grads, side_cells, terms, *, height
):
    units = bias.shape[0] // 4
    channels = columns.shape[0] - units
    spare = STACK - 3 * channels
    west, east = in_order(from_next, from_pair, EW[-1])
    west, east = west[:channels], east[:channels]
    slot = lax.broadcasted_iota(jnp.int32, (channels, LANES), 1) % STEP
    own = columns[:channels]
    outer = jnp.where(slot < 2, west, moved(east, 2))
    before = by_slot(slot, outer, moved(own, 1), moved(outer, 1), moved(own, 2))
    at = by_slot(slot, moved(outer, -1), own, own, moved(outer, 1))
    after = by_slot(slot, moved(own, -2), moved(outer, -1), moved(own, -1), outer)
    patches = jnp.concatenate([before, at, after], 0)
    ones_row = (lax.broadcasted_iota(jnp.int32, (spare, LANES), 0) == 0).astype(F32)
    stacks = [
        jnp.concatenate([moved(patches, -STEP * row_off), ones_row], 0).astype(BF16)
        for row_off in range(3)
    ]
    gates = jnp.broadcast_to(bias[...], (4 * units, LANES))
    for row_off in range(3):
        gates = gates + jnp.dot(
            weights[:, row_off * STACK : (row_off + 1) * STACK], stacks[row_off], preferred_element_type=F32
        )
    slot = slot[:units]
    here, west, east = columns[channels:], west[:units], east[:units]
    old = by_slot(slot, moved(west, -2), moved(here, 1), moved(here, 1), moved(east, 1))
    down = by_slot(slot, moved(west, -3), moved(here, -1), moved(here, -1), east)
    grad_cell = by_slot(slot, moved(west, -4), moved(here, -3), moved(here, -3), moved(east, -1))
    new_hidden, new, back, grads = gate_step(gates, old, down, grad_cell)
    side_cells[:units] = new_hidden
    side_cells[units : 2 * units] = new
    side_cells[2 * units :] = back
    side_grads[...] = grads.astype(BF16)
    lane = lax.broadcasted_iota(jnp.int32, grads.shape, 1)
    slot = lane % STEP
    inside = (lane >= STEP) & (lane < STEP * (height + 1)) & ((slot == 1) | (slot == 2))
    grads = jnp.where(inside, grads, 0.0).astype(BF16)
    for row_off in range(3):
        part = slice(row_off * STACK, (row_off + 1) * STACK)
        terms[part] = (
            inner_terms[part]
            + lax.dot_general(
                stacks[row_off], grads, (((1,), (1,)), ((), ())), preferred_element_type=F32
            )
        ).astype(BF16)


def backward_kernel(
    weights, grads, side_grads, side_cells, inner_hidden, inner_cell, inner_back,
    hidden, cell, grad_cell_prev, grad_frame, grad_hidden_prev,
    sums, rows,
):
    height = grads.shape[1] // LANES - 2
    units = hidden.shape[0] // height
    inputs = grad_frame.shape[0] // height
    channels = inputs + units
    lane = lax.broadcasted_iota(jnp.int32, (channels, LANES), 1)
    ends = (lane[:units] == 0) | (lane[:units] == LANES - 1)
    rows[: units * height] = inner_hidden[...].astype(F32)
    for n in range(height):
        at = pl.ds(n, units, stride=height)
        for i, (inner, out) in enumerate(((rows, rows), (inner_cell, cell), (inner_back, grad_cell_prev))):
            side = pltpu.roll(side_cells[i * units : (i + 1) * units], LANES - STEP * (n + 1) - 2, 1)
            out[at, :] = jnp.where(ends, side, inner[at, :])
    hidden[...] = rows[: units * height].astype(BF16)

    outer = jnp.dot(weights[...], side_grads[...], preferred_element_type=F32)
    parts = []
    for col_off in range(3):
        part = jnp.zeros((channels, LANES), F32)
        for row_off in range(3):
            start = (3 * row_off + col_off) * channels
            piece = outer[start : start + channels]
            part = part + moved(piece, -STEP * (2 - row_off))
        parts.append(part)
    slot = lane % STEP
    sides = jnp.where((slot == 1) | (slot == 2), parts[1], 0.0) + jnp.where(
        slot == 0,
        pltpu.roll(parts[0], LANES - 1, 1),
        jnp.where(
            slot == 1,
            pltpu.roll(parts[0], LANES - 2, 1),
            jnp.where(slot == 2, pltpu.roll(parts[2], 2, 1), pltpu.roll(parts[2], 1, 1)),
        ),
    )
    for place in range(0, height + 2, 2):
        cells = grads[:, place * LANES : (place + 2) * LANES]
        product = jnp.dot(weights[...], cells, preferred_element_type=F32)
        for half in range(2):
            for row_off in range(3):
                n = place + half + row_off - 2
                if not 0 <= n < height:
                    continue
                for col_off in range(3):
                    start = (3 * row_off + col_off) * channels
                    piece = product[start : start + channels, half * LANES : (half + 1) * LANES]
                    if row_off == 2:
                        sums[n, col_off] = piece
                    else:
                        sums[n, col_off] = sums[n, col_off] + piece
    edge = (lane < 2) | (lane >= LANES - 2)
    for n in range(height):
        total = sums[n, 1] + pltpu.roll(sums[n, 0], LANES - 1, 1) + pltpu.roll(sums[n, 2], 1, 1)
        total = total + jnp.where(edge, moved(sides, -STEP * n - 2), 0.0)
        rows[pl.ds(n, channels, stride=height), :] = total
    grad_frame[...] = rows[: inputs * height].astype(BF16)
    grad_hidden_prev[...] = rows[inputs * height :].astype(BF16)


def finish_kernel(total, kernel_step, bias_step):
    block = kernel_step.shape[0] // 3
    parts = [total[i * STACK : i * STACK + block].astype(F32) for i in range(3)]
    bias_grad = total[block : block + 8].astype(F32)[:1]
    norm = jnp.sqrt(sum(jnp.sum(part * part) for part in parts) + jnp.sum(bias_grad * bias_grad))
    factor = jnp.minimum(1.0, CLIP_NORM / norm)
    for i, part in enumerate(parts):
        kernel_step[i * block : (i + 1) * block] = part * factor
    bias_step[...] = bias_grad * factor


def sum_kernel(parts, *rest):
    copies = rest[-1]
    total = jnp.sum(parts[...].astype(F32), 0).astype(copies.dtype)
    copies[...] = jnp.broadcast_to(total[None], copies.shape)


def summed(parts, copies, kind, *after):
    return pl.pallas_call(
        sum_kernel,
        out_shape=jax.ShapeDtypeStruct((copies,) + parts.shape[1:], kind),
        in_specs=vmem(1) + [pl.BlockSpec(memory_space=pl.ANY)] * len(after),
        out_specs=vmem(1)[0],
        compiler_params=pltpu.CompilerParams(vmem_limit_bytes=8 * 2**20),
    )(parts, *after)


def exchanged(copies, axes):
    return lax.all_to_all(copies, axes, 0, 0, tiled=True)


def shape(rows, columns, kind):
    return jax.ShapeDtypeStruct((rows, columns), kind)


def called(kernel, outs, scratch, cost, *args, aliases={}):
    return pl.pallas_call(
        kernel,
        out_shape=tuple(outs),
        in_specs=vmem(len(args)),
        out_specs=tuple(vmem(len(outs))),
        scratch_shapes=scratch,
        input_output_aliases=aliases,
        compiler_params=pltpu.CompilerParams(vmem_limit_bytes=16 * 2**20),
        cost_estimate=pl.CostEstimate(flops=cost, bytes_accessed=2 * cost // 1000, transcendentals=0),
    )(*args)


def per_device(frame, hidden_prev, cell_prev, kernel, bias, grad_hidden, grad_cell):
    inputs, height, breadth = frame.shape
    units = hidden_prev.shape[0]
    channels = inputs + units
    gate_rows = kernel.shape[0]
    flat = (units * height, breadth)
    states = (cell_prev.reshape(flat), grad_hidden.reshape(flat), grad_cell.reshape(flat))

    strip = shape(2 * channels + 3 * units, breadth, BF16)
    blocks = (frame.reshape(inputs * height, breadth), hidden_prev.reshape(flat), *states)
    channel_rows = (channels * height, breadth)
    arrays = (frame, hidden_prev, cell_prev, grad_hidden, grad_cell)
    to_pair, to_next = pl.pallas_call(
        rows_kernel,
        out_shape=(strip, strip),
        in_specs=[pl.BlockSpec(memory_space=pl.ANY)] * 5,
        out_specs=tuple(vmem(2)),
        scratch_shapes=[
            pltpu.VMEM(channel_rows, F32),
            pltpu.VMEM(frame.shape, BF16),
            pltpu.VMEM(hidden_prev.shape, BF16),
            pltpu.VMEM((2, 3, units, breadth), F32),
            pltpu.SemaphoreType.DMA((8,)),
        ],
        compiler_params=pltpu.CompilerParams(vmem_limit_bytes=60 * 2**20),
        cost_estimate=pl.CostEstimate(flops=1_000_000, bytes_accessed=1_000_000, transcendentals=0),
    )(*arrays)
    edge = shape(channels + units, LANES, F32)
    columns, stacked = called(
        functools.partial(columns_kernel, height=height),
        [edge, shape(STACK, height * breadth, BF16)],
        [pltpu.VMEM(channel_rows, F32)],
        1_000_000,
        *blocks,
    )
    rows = swapped(to_pair, to_next, NS)
    sent = shape(-(-channels // 16) * 16, LANES, BF16)
    columns, to_next, to_pair = called(
        functools.partial(corners_kernel, height=height, units=units), [edge, sent, sent], [], 100_000, columns, *rows
    )
    sides = swapped(to_pair, to_next, EW)
    bias = bias[:, None]
    field = shape(*flat, F32)
    cube = jax.ShapeDtypeStruct((units, height, breadth), F32)
    inner_hidden, inner_cell, inner_back, grads, inner_terms, weights = pl.pallas_call(
        forward_kernel,
        out_shape=(
            shape(*flat, BF16),
            cube,
            cube,
            shape(gate_rows, (height + 2) * breadth, BF16),
            shape(3 * STACK, gate_rows, F32),
            shape(gate_rows, 3 * STACK, BF16),
        ),
        in_specs=vmem(8),
        out_specs=tuple([pl.BlockSpec(memory_space=pl.ANY)] * 3 + vmem(3)),
        scratch_shapes=[
            pltpu.VMEM(flat, F32),
            pltpu.VMEM(flat, BF16),
            pltpu.VMEM(cube.shape, F32),
            pltpu.VMEM(cube.shape, F32),
            pltpu.SemaphoreType.DMA((5,)),
        ],
        compiler_params=pltpu.CompilerParams(vmem_limit_bytes=16 * 2**20),
        cost_estimate=pl.CostEstimate(flops=1_400_000_000, bytes_accessed=4_000_000, transcendentals=700_000),
    )(stacked, *rows, kernel.T, bias, *states)
    side_grads, side_cells, terms = called(
        functools.partial(sides_kernel, height=height),
        [shape(gate_rows, LANES, BF16), shape(3 * units, LANES, F32), shape(3 * STACK, gate_rows, BF16)],
        [],
        100_000_000,
        columns,
        *sides,
        weights,
        bias,
        inner_terms,
    )

    plane = lax.axis_size(PLANE)
    low, high = lax.axis_size("z_lo"), lax.axis_size("z_hi")
    mine = exchanged(terms.reshape(plane, -1, gate_rows), PLANE)
    mine = exchanged(summed(mine, low, F32), "z_lo")
    mine = exchanged(summed(mine, high, F32), "z_hi")
    mine = summed(mine, plane, BF16)
    total = exchanged(mine, PLANE).reshape(3 * STACK, gate_rows)
    hidden, cell, grad_cell_prev, grad_frame, grad_hidden_prev = called(
        backward_kernel,
        [shape(*flat, BF16), field, field, shape(inputs * height, breadth, BF16), shape(*flat, BF16)],
        [pltpu.VMEM((height, 3, channels, breadth), F32), pltpu.VMEM((channels * height, breadth), F32)],
        764_000_000,
        kernel.T,
        grads,
        side_grads,
        side_cells,
        inner_hidden,
        inner_cell.reshape(flat),
        inner_back.reshape(flat),
        aliases={4: 0, 5: 1, 6: 2},
    )
    kernel_step, bias_step = called(
        finish_kernel, [shape(9 * channels, gate_rows, F32), shape(1, gate_rows, F32)], [], 1_000_000, total
    )
    whole = (units, height, breadth)
    return (
        hidden.reshape(whole),
        cell.reshape(whole),
        grad_frame.reshape(frame.shape),
        grad_hidden_prev.reshape(whole),
        grad_cell_prev.reshape(whole),
        kernel_step.T,
        bias_step.reshape(gate_rows),
    )


def solution(mesh):
    mesh = Mesh(mesh.devices.reshape(4, 4, 2, 4, 2, 2), EW + NS)
    grid = P(None, NS, EW)
    return jax.shard_map(
        per_device,
        mesh=mesh,
        in_specs=(grid, grid, grid, P(), P(), grid, grid),
        out_specs=(grid, grid, grid, grid, grid, P(), P()),
        check_vma=False,
    )
```

```python
import functools

import jax
import jax.numpy as jnp
from jax import lax
from jax.experimental import pallas as pl
from jax.experimental.pallas import tpu as pltpu
from jax.sharding import Mesh, PartitionSpec as P

CLIP_NORM = 100.0
EW = ("z_hi", "z_lo", "x_hi")
NS = ("y", "x_lo", "core")
PLANE = ("x_hi", "y", "x_lo", "core")
LANES = 128
STACK = 256
STEP = 6
BF16 = jnp.bfloat16
F32 = jnp.float32


def vmem(count):
    return [pl.BlockSpec(memory_space=pltpu.VMEM)] * count


def swapped(to_pair, to_next, axes):
    count = lax.axis_size(axes)
    pairs = [(i, i ^ 1) for i in range(count) if i ^ 1 < count]
    across = [(i, (i + 1 ^ 1) - 1) for i in range(1, count - 1)]
    other = lax.ppermute(to_next, axes, across)
    return other, lax.ppermute(to_pair, axes, pairs)


def in_order(from_next, from_pair, axis):
    first = lax.axis_index(axis) == 0
    from_pair = from_pair[...].astype(F32)
    from_next = from_next[...].astype(F32)
    return jnp.where(first, from_next, from_pair), jnp.where(first, from_pair, from_next)


def sigmoid(x):
    return 0.5 * jnp.tanh(0.5 * x) + 0.5


def rows_kernel(
    frame, hidden_prev, cell_prev, grad_hidden, grad_cell, to_pair, to_next, joined, frame_here, hidden_here, ends, sems
):
    inputs, height, _ = frame_here.shape
    copies = [
        pltpu.make_async_copy(frame, frame_here, sems.at[0]),
        pltpu.make_async_copy(hidden_prev, hidden_here, sems.at[1]),
    ]
    for i, state in enumerate((cell_prev, grad_hidden, grad_cell)):
        for j, n in enumerate((0, height - 1)):
            copies.append(pltpu.make_async_copy(state.at[:, n, :], ends.at[j, i], sems.at[2 + 2 * i + j]))
    for copy in copies:
        copy.start()
    channels = joined.shape[0] // height
    copies[0].wait()
    joined[: inputs * height] = frame_here[...].astype(F32).reshape(-1, LANES)
    copies[1].wait()
    joined[inputs * height :] = hidden_here[...].astype(F32).reshape(-1, LANES)
    for copy in copies[2:]:
        copy.wait()
    strips = []
    for j, rows in enumerate(((0, 1), (height - 2, height - 1))):
        parts = [joined[pl.ds(n, channels, stride=height), :] for n in rows]
        strips.append(jnp.concatenate(parts + [ends[j, i] for i in range(3)], 0))
    first = lax.axis_index(NS[-1]) == 0
    to_pair[...] = jnp.where(first, strips[1], strips[0]).astype(BF16)
    to_next[...] = jnp.where(first, strips[0], strips[1]).astype(BF16)


def put_channels(tile, row, place):
    lane = lax.broadcasted_iota(jnp.int32, tile.shape, 1)
    return jnp.where(lane // STEP == place, pltpu.roll(row, (STEP * place + 2) % LANES, 1), tile)


def put_state(tile, row, place, slot):
    lane = lax.broadcasted_iota(jnp.int32, tile.shape, 1)
    start = STEP * place + slot
    return jnp.where(lane // 2 == start // 2, pltpu.roll(row, (start + 1) % LANES, 1), tile)


def stack_of(row):
    spare = STACK - 3 * row.shape[0]
    ones_row = (lax.broadcasted_iota(jnp.int32, (spare, LANES), 0) == 0).astype(F32)
    return jnp.concatenate([pltpu.roll(row, 1, 1), row, pltpu.roll(row, LANES - 1, 1), ones_row], 0).astype(BF16)


def columns_kernel(frame, hidden_prev, cell_prev, grad_hidden, grad_cell, columns, stacked, joined, *, height):
    joined[: frame.shape[0]] = frame[...].astype(F32)
    joined[frame.shape[0] :] = hidden_prev[...].astype(F32)
    channels = joined.shape[0] // height
    units = cell_prev.shape[0] // height
    tile = jnp.zeros((channels, LANES), F32)
    states = jnp.zeros((units, LANES), F32)
    for n in range(height):
        at = pl.ds(n, units, stride=height)
        row = joined[pl.ds(n, channels, stride=height), :]
        stacked[:, n * LANES : (n + 1) * LANES] = stack_of(row)
        tile = put_channels(tile, row, n + 2)
        for i, state in enumerate((cell_prev, grad_hidden, grad_cell)):
            states = put_state(states, state[at, :], n + 1, 2 * i)
    columns[:channels] = tile
    columns[channels:] = states


def moved(x, lanes):
    return pltpu.roll(x, lanes % LANES, 1) if lanes else x


def by_slot(slot, *choices):
    out = choices[-1]
    for i in range(len(choices) - 2, -1, -1):
        out = jnp.where(slot == i, choices[i], out)
    return out


def corners_kernel(columns, from_next, from_pair, out, to_next, to_pair, *, height, units):
    channels = columns.shape[0] - units
    top, bottom = in_order(from_next, from_pair, NS[-1])
    tile = columns[:channels]
    states = columns[channels:]
    for rows, place, state_place in ((top, 0, 0), (bottom, height + 2, height + 1)):
        for i in range(2):
            tile = put_channels(tile, rows[i * channels : (i + 1) * channels], place + i)
        for i in range(3):
            start = 2 * channels + i * units
            states = put_state(states, rows[start : start + units], state_place, 2 * i)
    out[:channels] = tile
    out[channels:] = states
    slot = lax.broadcasted_iota(jnp.int32, (channels, LANES), 1) % STEP
    blank = jnp.zeros((channels - units, LANES), F32)
    east = [jnp.concatenate([moved(states, k), blank], 0) for k in (2, 1, 0)]
    west = [jnp.concatenate([moved(states, k), blank], 0) for k in (1, 0, -1)]
    east = by_slot(slot, tile, tile, *east)
    west = by_slot(slot, moved(tile, -2), moved(tile, -2), *west)
    spare = jnp.zeros((to_pair.shape[0] - channels, LANES), F32)
    first = lax.axis_index(EW[-1]) == 0
    to_pair[...] = jnp.concatenate([jnp.where(first, east, west), spare], 0).astype(BF16)
    to_next[...] = jnp.concatenate([jnp.where(first, west, east), spare], 0).astype(BF16)


def gate_step(gates, old, down, grad_cell):
    units = old.shape[0]
    input_gate = sigmoid(gates[:units])
    forget_gate = sigmoid(gates[units : 2 * units])
    cand_gate = jnp.tanh(gates[2 * units : 3 * units])
    output_gate = sigmoid(gates[3 * units :])
    new = forget_gate * old + input_gate * cand_gate
    new_tanh = jnp.tanh(new)
    cell_grad = grad_cell + down * output_gate * (1.0 - new_tanh * new_tanh)
    grads = [
        cell_grad * cand_gate * input_gate * (1.0 - input_gate),
        cell_grad * old * forget_gate * (1.0 - forget_gate),
        cell_grad * input_gate * (1.0 - cand_gate * cand_gate),
        down * new_tanh * output_gate * (1.0 - output_gate),
    ]
    return output_gate * new_tanh, new, cell_grad * forget_gate, jnp.concatenate(grads, 0)


def forward_kernel(
    stacked, from_next, from_pair, kernel, bias, cell_prev, grad_hidden, grad_cell,
    hidden, cell, grad_cell_prev, grads, terms, weights,
    hidden_rows, hidden_here, cell_here, back_here, sems,
):
    depth = kernel.shape[0] // 3
    blank = jnp.zeros((STACK - depth, kernel.shape[1]), F32)
    for row_off in range(3):
        part = kernel[...].astype(F32)[row_off * depth : (row_off + 1) * depth]
        weights[:, row_off * STACK : (row_off + 1) * STACK] = jnp.concatenate([part, blank], 0).T.astype(BF16)
    units = bias.shape[0] // 4
    height = cell_prev.shape[0] // units
    channels = (from_pair.shape[0] - 3 * units) // 2
    top, bottom = in_order(from_next, from_pair, NS[-1])
    north = [stack_of(top[i * channels : (i + 1) * channels]) for i in range(2)]
    south = [stack_of(bottom[i * channels : (i + 1) * channels]) for i in range(2)]

    def two_rows(place):
        if 2 <= place <= height:
            return stacked[:, (place - 2) * LANES : place * LANES]
        outer = [None] * (height + 4)
        outer[:2], outer[-2:] = north, south
        outer[2], outer[-3] = stacked[:, :LANES], stacked[:, (height - 1) * LANES :]
        return jnp.concatenate(outer[place : place + 2], 1)

    def copy_out(half):
        rows = pl.ds(half * (height // 2), height // 2)
        return [
            pltpu.make_async_copy(here.at[:, rows, :], out.at[:, rows, :], sems.at[2 * half + i])
            for i, (here, out) in enumerate(((cell_here, cell), (back_here, grad_cell_prev)))
        ]

    cell_rows = cell_here.reshape(units * height, LANES)
    back_rows = back_here.reshape(units * height, LANES)
    bias_cells = jnp.broadcast_to(bias[...], (4 * units, LANES))
    lane = lax.broadcasted_iota(jnp.int32, (4 * units, LANES), 1)
    middle = (lane > 0) & (lane < LANES - 1)
    for pair in range(height // 2 + 1):
        sums = jnp.zeros((4 * units, 2 * LANES), F32)
        for row_off in range(3):
            sums = sums + jnp.dot(
                weights[:, row_off * STACK : (row_off + 1) * STACK],
                two_rows(2 * pair + row_off),
                preferred_element_type=F32,
            )
        for half in range(2):
            place = 2 * pair + half
            gates = sums[:, half * LANES : (half + 1) * LANES] + bias_cells
            inside = 0 < place <= height
            if inside:
                at = pl.ds(place - 1, units, stride=height)
                states = [cell_prev[at, :], grad_hidden[at, :], grad_cell[at, :]]
            else:
                rows = bottom if place else top
                states = [rows[2 * channels + i * units : 2 * channels + (i + 1) * units] for i in range(3)]
            new_hidden, new, down, row_grads = gate_step(gates, *states)
            grads[:, place * LANES : (place + 1) * LANES] = jnp.where(middle, row_grads, 0.0).astype(BF16)
            if inside:
                hidden_rows[at, :] = new_hidden
                cell_rows[at, :] = new
                back_rows[at, :] = down
        if pair == height // 4:
            for copy in copy_out(0):
                copy.start()
    hidden_here[...] = hidden_rows[...].astype(BF16)
    hidden_copy = pltpu.make_async_copy(hidden_here, hidden, sems.at[4])
    copies = copy_out(0) + copy_out(1) + [hidden_copy]
    for copy in copies[2:]:
        copy.start()
    own = grads[:, LANES : (height + 1) * LANES]
    for row_off in range(3):
        if row_off == 0:
            rows = jnp.concatenate([north[1], stacked[:, : (height - 1) * LANES]], 1)
        elif row_off == 1:
            rows = stacked[...]
        else:
            rows = jnp.concatenate([stacked[:, LANES:], south[0]], 1)
        terms[row_off * STACK : (row_off + 1) * STACK] = lax.dot_general(
            rows, own, (((1,), (1,)), ((), ())), preferred_element_type=F32
        )
    for copy in copies:
        copy.wait()


def sides_kernel(
    columns, from_next, from_pair, weights, bias, inner_terms, side_grads, side_cells, terms, *, height
):
    units = bias.shape[0] // 4
    channels = columns.shape[0] - units
    spare = STACK - 3 * channels
    west, east = in_order(from_next, from_pair, EW[-1])
    west, east = west[:channels], east[:channels]
    slot = lax.broadcasted_iota(jnp.int32, (channels, LANES), 1) % STEP
    own = columns[:channels]
    outer = jnp.where(slot < 2, west, moved(east, 2))
    before = by_slot(slot, outer, moved(own, 1), moved(outer, 1), moved(own, 2))
    at = by_slot(slot, moved(outer, -1), own, own, moved(outer, 1))
    after = by_slot(slot, moved(own, -2), moved(outer, -1), moved(own, -1), outer)
    patches = jnp.concatenate([before, at, after], 0)
    ones_row = (lax.broadcasted_iota(jnp.int32, (spare, LANES), 0) == 0).astype(F32)
    stacks = [
        jnp.concatenate([moved(patches, -STEP * row_off), ones_row], 0).astype(BF16)
        for row_off in range(3)
    ]
    gates = jnp.broadcast_to(bias[...], (4 * units, LANES))
    for row_off in range(3):
        gates = gates + jnp.dot(
            weights[:, row_off * STACK : (row_off + 1) * STACK], stacks[row_off], preferred_element_type=F32
        )
    slot = slot[:units]
    here, west, east = columns[channels:], west[:units], east[:units]
    old = by_slot(slot, moved(west, -2), moved(here, 1), moved(here, 1), moved(east, 1))
    down = by_slot(slot, moved(west, -3), moved(here, -1), moved(here, -1), east)
    grad_cell = by_slot(slot, moved(west, -4), moved(here, -3), moved(here, -3), moved(east, -1))
    new_hidden, new, back, grads = gate_step(gates, old, down, grad_cell)
    side_cells[:units] = new_hidden
    side_cells[units : 2 * units] = new
    side_cells[2 * units :] = back
    side_grads[...] = grads.astype(BF16)
    lane = lax.broadcasted_iota(jnp.int32, grads.shape, 1)
    slot = lane % STEP
    inside = (lane >= STEP) & (lane < STEP * (height + 1)) & ((slot == 1) | (slot == 2))
    grads = jnp.where(inside, grads, 0.0).astype(BF16)
    for row_off in range(3):
        total = inner_terms[row_off * STACK : (row_off + 1) * STACK] + lax.dot_general(
            stacks[row_off], grads, (((1,), (1,)), ((), ())), preferred_element_type=F32
        )
        for half in range(2):
            start = (3 * half + row_off) * STACK
            terms[start : start + STACK] = total[:, half * LANES : (half + 1) * LANES].astype(BF16)


def backward_kernel(
    weights, grads, side_grads, side_cells, inner_hidden, inner_cell, inner_back,
    hidden, cell, grad_cell_prev, grad_frame, grad_hidden_prev,
    sums, rows,
):
    height = grads.shape[1] // LANES - 2
    units = hidden.shape[0] // height
    inputs = grad_frame.shape[0] // height
    channels = inputs + units
    lane = lax.broadcasted_iota(jnp.int32, (channels, LANES), 1)
    ends = (lane[:units] == 0) | (lane[:units] == LANES - 1)
    rows[: units * height] = inner_hidden[...].astype(F32)
    for n in range(height):
        at = pl.ds(n, units, stride=height)
        for i, (inner, out) in enumerate(((rows, rows), (inner_cell, cell), (inner_back, grad_cell_prev))):
            side = pltpu.roll(side_cells[i * units : (i + 1) * units], LANES - STEP * (n + 1) - 2, 1)
            out[at, :] = jnp.where(ends, side, inner[at, :])
    hidden[...] = rows[: units * height].astype(BF16)

    outer = jnp.dot(weights[...], side_grads[...], preferred_element_type=F32)
    parts = []
    for col_off in range(3):
        part = jnp.zeros((channels, LANES), F32)
        for row_off in range(3):
            start = (3 * row_off + col_off) * channels
            piece = outer[start : start + channels]
            part = part + moved(piece, -STEP * (2 - row_off))
        parts.append(part)
    slot = lane % STEP
    sides = jnp.where((slot == 1) | (slot == 2), parts[1], 0.0) + jnp.where(
        slot == 0,
        pltpu.roll(parts[0], LANES - 1, 1),
        jnp.where(
            slot == 1,
            pltpu.roll(parts[0], LANES - 2, 1),
            jnp.where(slot == 2, pltpu.roll(parts[2], 2, 1), pltpu.roll(parts[2], 1, 1)),
        ),
    )
    for place in range(0, height + 2, 2):
        cells = grads[:, place * LANES : (place + 2) * LANES]
        product = jnp.dot(weights[...], cells, preferred_element_type=F32)
        for half in range(2):
            for row_off in range(3):
                n = place + half + row_off - 2
                if not 0 <= n < height:
                    continue
                for col_off in range(3):
                    start = (3 * row_off + col_off) * channels
                    piece = product[start : start + channels, half * LANES : (half + 1) * LANES]
                    if row_off == 2:
                        sums[n, col_off] = piece
                    else:
                        sums[n, col_off] = sums[n, col_off] + piece
    edge = (lane < 2) | (lane >= LANES - 2)
    for n in range(height):
        total = sums[n, 1] + pltpu.roll(sums[n, 0], LANES - 1, 1) + pltpu.roll(sums[n, 2], 1, 1)
        total = total + jnp.where(edge, moved(sides, -STEP * n - 2), 0.0)
        rows[pl.ds(n, channels, stride=height), :] = total
    grad_frame[...] = rows[: inputs * height].astype(BF16)
    grad_hidden_prev[...] = rows[inputs * height :].astype(BF16)


def finish_kernel(total, kernel_step, bias_step, scaled, sems):
    block = kernel_step.shape[0] // 3
    halves = [total[half * 3 * STACK : (half + 1) * 3 * STACK].astype(F32) for half in range(2)]
    whole = jnp.concatenate(halves, 1)
    parts = [whole[i * STACK : i * STACK + block] for i in range(3)]
    bias_grad = whole[block : block + 1]
    norm = jnp.sqrt(sum(jnp.sum(part * part) for part in parts) + jnp.sum(bias_grad * bias_grad))
    factor = jnp.minimum(1.0, CLIP_NORM / norm)
    copies = []
    for i, part in enumerate(parts):
        rows = pl.ds(i * block, block)
        scaled[rows] = part * factor
        copies.append(pltpu.make_async_copy(scaled.at[rows], kernel_step.at[rows], sems.at[i]))
        copies[-1].start()
    bias_step[...] = bias_grad * factor
    for copy in copies:
        copy.wait()


def sum_kernel(parts, copies):
    total = jnp.sum(parts[...].astype(F32), 0).astype(copies.dtype)
    copies[...] = jnp.broadcast_to(total[None], copies.shape)


def summed(parts, copies, kind):
    return pl.pallas_call(
        sum_kernel,
        out_shape=jax.ShapeDtypeStruct((copies,) + parts.shape[1:], kind),
        in_specs=vmem(1),
        out_specs=vmem(1)[0],
        compiler_params=pltpu.CompilerParams(vmem_limit_bytes=8 * 2**20),
    )(parts)


def spread_kernel(parts, copies, few, sems):
    total = jnp.sum(parts[...], 0).astype(few.dtype)
    few[...] = jnp.broadcast_to(total[None], few.shape)
    count = few.shape[0]
    moves = [
        pltpu.make_async_copy(few, copies.at[pl.ds(i * count, count)], sems.at[i])
        for i in range(copies.shape[0] // count)
    ]
    for move in moves:
        move.start()
    for move in moves:
        move.wait()


def spread(parts, copies, kind):
    few = max(copies // 8, 1)
    return pl.pallas_call(
        spread_kernel,
        out_shape=jax.ShapeDtypeStruct((copies,) + parts.shape[1:], kind),
        in_specs=vmem(1),
        out_specs=pl.BlockSpec(memory_space=pl.ANY),
        scratch_shapes=[
            pltpu.VMEM((few,) + parts.shape[1:], kind),
            pltpu.SemaphoreType.DMA((copies // few,)),
        ],
        compiler_params=pltpu.CompilerParams(vmem_limit_bytes=8 * 2**20),
    )(parts)


def exchanged(copies, axes):
    return lax.all_to_all(copies, axes, 0, 0, tiled=True)


def shape(rows, columns, kind):
    return jax.ShapeDtypeStruct((rows, columns), kind)


def called(kernel, outs, scratch, cost, *args, aliases={}):
    return pl.pallas_call(
        kernel,
        out_shape=tuple(outs),
        in_specs=vmem(len(args)),
        out_specs=tuple(vmem(len(outs))),
        scratch_shapes=scratch,
        input_output_aliases=aliases,
        compiler_params=pltpu.CompilerParams(vmem_limit_bytes=16 * 2**20),
        cost_estimate=pl.CostEstimate(flops=cost, bytes_accessed=2 * cost // 1000, transcendentals=0),
    )(*args)


def per_device(frame, hidden_prev, cell_prev, kernel, bias, grad_hidden, grad_cell):
    inputs, height, breadth = frame.shape
    units = hidden_prev.shape[0]
    channels = inputs + units
    gate_rows = kernel.shape[0]
    flat = (units * height, breadth)
    states = (cell_prev.reshape(flat), grad_hidden.reshape(flat), grad_cell.reshape(flat))

    strip = shape(2 * channels + 3 * units, breadth, BF16)
    blocks = (frame.reshape(inputs * height, breadth), hidden_prev.reshape(flat), *states)
    channel_rows = (channels * height, breadth)
    arrays = (frame, hidden_prev, cell_prev, grad_hidden, grad_cell)
    to_pair, to_next = pl.pallas_call(
        rows_kernel,
        out_shape=(strip, strip),
        in_specs=[pl.BlockSpec(memory_space=pl.ANY)] * 5,
        out_specs=tuple(vmem(2)),
        scratch_shapes=[
            pltpu.VMEM(channel_rows, F32),
            pltpu.VMEM(frame.shape, BF16),
            pltpu.VMEM(hidden_prev.shape, BF16),
            pltpu.VMEM((2, 3, units, breadth), F32),
            pltpu.SemaphoreType.DMA((8,)),
        ],
        compiler_params=pltpu.CompilerParams(vmem_limit_bytes=60 * 2**20),
        cost_estimate=pl.CostEstimate(flops=1_000_000, bytes_accessed=1_000_000, transcendentals=0),
    )(*arrays)
    edge = shape(channels + units, LANES, F32)
    columns, stacked = called(
        functools.partial(columns_kernel, height=height),
        [edge, shape(STACK, height * breadth, BF16)],
        [pltpu.VMEM(channel_rows, F32)],
        1_000_000,
        *blocks,
    )
    rows = swapped(to_pair, to_next, NS)
    sent = shape(-(-channels // 16) * 16, LANES, BF16)
    columns, to_next, to_pair = called(
        functools.partial(corners_kernel, height=height, units=units), [edge, sent, sent], [], 100_000, columns, *rows
    )
    sides = swapped(to_pair, to_next, EW)
    bias = bias[:, None]
    field = shape(*flat, F32)
    cube = jax.ShapeDtypeStruct((units, height, breadth), F32)
    inner_hidden, inner_cell, inner_back, grads, inner_terms, weights = pl.pallas_call(
        forward_kernel,
        out_shape=(
            shape(*flat, BF16),
            cube,
            cube,
            shape(gate_rows, (height + 2) * breadth, BF16),
            shape(3 * STACK, gate_rows, F32),
            shape(gate_rows, 3 * STACK, BF16),
        ),
        in_specs=vmem(8),
        out_specs=tuple([pl.BlockSpec(memory_space=pl.ANY)] * 3 + vmem(3)),
        scratch_shapes=[
            pltpu.VMEM(flat, F32),
            pltpu.VMEM(flat, BF16),
            pltpu.VMEM(cube.shape, F32),
            pltpu.VMEM(cube.shape, F32),
            pltpu.SemaphoreType.DMA((5,)),
        ],
        compiler_params=pltpu.CompilerParams(vmem_limit_bytes=16 * 2**20),
        cost_estimate=pl.CostEstimate(flops=1_400_000_000, bytes_accessed=4_000_000, transcendentals=700_000),
    )(stacked, *rows, kernel.T, bias, *states)
    side_grads, side_cells, terms = called(
        functools.partial(sides_kernel, height=height),
        [shape(gate_rows, LANES, BF16), shape(3 * units, LANES, F32), shape(6 * STACK, LANES, BF16)],
        [],
        100_000_000,
        columns,
        *sides,
        weights,
        bias,
        inner_terms,
    )

    plane = lax.axis_size(PLANE)
    low, high = lax.axis_size("z_lo"), lax.axis_size("z_hi")
    mine = exchanged(terms.reshape(plane, -1, LANES), PLANE)
    mine = exchanged(summed(mine, low, F32), "z_lo")
    mine = exchanged(summed(mine, high, F32), "z_hi")
    mine = spread(mine, plane, BF16)
    total = exchanged(mine, PLANE).reshape(6 * STACK, LANES)
    hidden, cell, grad_cell_prev, grad_frame, grad_hidden_prev = called(
        backward_kernel,
        [shape(*flat, BF16), field, field, shape(inputs * height, breadth, BF16), shape(*flat, BF16)],
        [pltpu.VMEM((height, 3, channels, breadth), F32), pltpu.VMEM((channels * height, breadth), F32)],
        764_000_000,
        kernel.T,
        grads,
        side_grads,
        side_cells,
        inner_hidden,
        inner_cell.reshape(flat),
        inner_back.reshape(flat),
        aliases={4: 0, 5: 1, 6: 2},
    )
    kernel_step, bias_step = pl.pallas_call(
        finish_kernel,
        out_shape=(shape(9 * channels, gate_rows, F32), shape(1, gate_rows, F32)),
        in_specs=vmem(1),
        out_specs=(pl.BlockSpec(memory_space=pl.ANY), vmem(1)[0]),
        scratch_shapes=[pltpu.VMEM((9 * channels, gate_rows), F32), pltpu.SemaphoreType.DMA((3,))],
        compiler_params=pltpu.CompilerParams(vmem_limit_bytes=8 * 2**20),
    )(total)
    whole = (units, height, breadth)
    return (
        hidden.reshape(whole),
        cell.reshape(whole),
        grad_frame.reshape(frame.shape),
        grad_hidden_prev.reshape(whole),
        grad_cell_prev.reshape(whole),
        kernel_step.T,
        bias_step.reshape(gate_rows),
    )


def solution(mesh):
    mesh = Mesh(mesh.devices.reshape(4, 4, 2, 4, 2, 2), EW + NS)
    grid = P(None, NS, EW)
    return jax.shard_map(
        per_device,
        mesh=mesh,
        in_specs=(grid, grid, grid, P(), P(), grid, grid),
        out_specs=(grid, grid, grid, grid, grid, P(), P()),
        check_vma=False,
    )
```

```python
import functools

import jax
import jax.numpy as jnp
from jax import lax
from jax.experimental import pallas as pl
from jax.experimental.pallas import tpu as pltpu
from jax.sharding import Mesh, PartitionSpec as P

CLIP_NORM = 100.0
EW = ("z_hi", "z_lo", "x_hi")
NS = ("y", "x_lo", "core")
PLANE = ("x_hi", "y", "x_lo", "core")
LANES = 128
STACK = 256
STEP = 6
BF16 = jnp.bfloat16
F32 = jnp.float32


def vmem(count):
    return [pl.BlockSpec(memory_space=pltpu.VMEM)] * count


def swapped(to_pair, to_next, axes):
    count = lax.axis_size(axes)
    pairs = [(i, i ^ 1) for i in range(count) if i ^ 1 < count]
    across = [(i, (i + 1 ^ 1) - 1) for i in range(1, count - 1)]
    other = lax.ppermute(to_next, axes, across)
    return other, lax.ppermute(to_pair, axes, pairs)


def in_order(from_next, from_pair, axis):
    first = lax.axis_index(axis) == 0
    from_pair = from_pair[...].astype(F32)
    from_next = from_next[...].astype(F32)
    return jnp.where(first, from_next, from_pair), jnp.where(first, from_pair, from_next)


def sigmoid(x):
    return 0.5 * jnp.tanh(0.5 * x) + 0.5


def rows_kernel(
    frame, hidden_prev, cell_prev, grad_hidden, grad_cell, to_pair, to_next, joined, frame_here, hidden_here, ends, sems
):
    inputs, height, _ = frame_here.shape
    copies = [
        pltpu.make_async_copy(frame, frame_here, sems.at[0]),
        pltpu.make_async_copy(hidden_prev, hidden_here, sems.at[1]),
    ]
    for i, state in enumerate((cell_prev, grad_hidden, grad_cell)):
        for j, n in enumerate((0, height - 1)):
            copies.append(pltpu.make_async_copy(state.at[:, n, :], ends.at[j, i], sems.at[2 + 2 * i + j]))
    for copy in copies:
        copy.start()
    channels = joined.shape[0] // height
    copies[0].wait()
    joined[: inputs * height] = frame_here[...].astype(F32).reshape(-1, LANES)
    copies[1].wait()
    joined[inputs * height :] = hidden_here[...].astype(F32).reshape(-1, LANES)
    for copy in copies[2:]:
        copy.wait()
    strips = []
    for j, rows in enumerate(((0, 1), (height - 2, height - 1))):
        parts = [joined[pl.ds(n, channels, stride=height), :] for n in rows]
        strips.append(jnp.concatenate(parts + [ends[j, i] for i in range(3)], 0))
    first = lax.axis_index(NS[-1]) == 0
    to_pair[...] = jnp.where(first, strips[1], strips[0]).astype(BF16)
    to_next[...] = jnp.where(first, strips[0], strips[1]).astype(BF16)


def put_channels(tile, row, place):
    lane = lax.broadcasted_iota(jnp.int32, tile.shape, 1)
    return jnp.where(lane // STEP == place, pltpu.roll(row, (STEP * place + 2) % LANES, 1), tile)


def put_state(tile, row, place, slot):
    lane = lax.broadcasted_iota(jnp.int32, tile.shape, 1)
    start = STEP * place + slot
    return jnp.where(lane // 2 == start // 2, pltpu.roll(row, (start + 1) % LANES, 1), tile)


def stack_of(row):
    spare = STACK - 3 * row.shape[0]
    ones_row = (lax.broadcasted_iota(jnp.int32, (spare, LANES), 0) == 0).astype(F32)
    return jnp.concatenate([pltpu.roll(row, 1, 1), row, pltpu.roll(row, LANES - 1, 1), ones_row], 0).astype(BF16)


def columns_kernel(frame, hidden_prev, cell_prev, grad_hidden, grad_cell, columns, stacked, joined, *, height):
    joined[: frame.shape[0]] = frame[...].astype(F32)
    joined[frame.shape[0] :] = hidden_prev[...].astype(F32)
    channels = joined.shape[0] // height
    units = cell_prev.shape[0] // height
    tile = jnp.zeros((channels, LANES), F32)
    states = jnp.zeros((units, LANES), F32)
    for n in range(height):
        at = pl.ds(n, units, stride=height)
        row = joined[pl.ds(n, channels, stride=height), :]
        stacked[:, n * LANES : (n + 1) * LANES] = stack_of(row)
        tile = put_channels(tile, row, n + 2)
        for i, state in enumerate((cell_prev, grad_hidden, grad_cell)):
            states = put_state(states, state[at, :], n + 1, 2 * i)
    columns[:channels] = tile
    columns[channels:] = states


def moved(x, lanes):
    return pltpu.roll(x, lanes % LANES, 1) if lanes else x


def by_slot(slot, *choices):
    out = choices[-1]
    for i in range(len(choices) - 2, -1, -1):
        out = jnp.where(slot == i, choices[i], out)
    return out


def corners_kernel(columns, from_next, from_pair, out, to_next, to_pair, *, height, units):
    channels = columns.shape[0] - units
    top, bottom = in_order(from_next, from_pair, NS[-1])
    tile = columns[:channels]
    states = columns[channels:]
    for rows, place, state_place in ((top, 0, 0), (bottom, height + 2, height + 1)):
        for i in range(2):
            tile = put_channels(tile, rows[i * channels : (i + 1) * channels], place + i)
        for i in range(3):
            start = 2 * channels + i * units
            states = put_state(states, rows[start : start + units], state_place, 2 * i)
    out[:channels] = tile
    out[channels:] = states
    slot = lax.broadcasted_iota(jnp.int32, (channels, LANES), 1) % STEP
    blank = jnp.zeros((channels - units, LANES), F32)
    east = [jnp.concatenate([moved(states, k), blank], 0) for k in (2, 1, 0)]
    west = [jnp.concatenate([moved(states, k), blank], 0) for k in (1, 0, -1)]
    east = by_slot(slot, tile, tile, *east)
    west = by_slot(slot, moved(tile, -2), moved(tile, -2), *west)
    spare = jnp.zeros((to_pair.shape[0] - channels, LANES), F32)
    first = lax.axis_index(EW[-1]) == 0
    to_pair[...] = jnp.concatenate([jnp.where(first, east, west), spare], 0).astype(BF16)
    to_next[...] = jnp.concatenate([jnp.where(first, west, east), spare], 0).astype(BF16)


def gate_step(gates, old, down, grad_cell):
    units = old.shape[0]
    input_gate = sigmoid(gates[:units])
    forget_gate = sigmoid(gates[units : 2 * units])
    cand_gate = jnp.tanh(gates[2 * units : 3 * units])
    output_gate = sigmoid(gates[3 * units :])
    new = forget_gate * old + input_gate * cand_gate
    new_tanh = jnp.tanh(new)
    cell_grad = grad_cell + down * output_gate * (1.0 - new_tanh * new_tanh)
    grads = [
        cell_grad * cand_gate * input_gate * (1.0 - input_gate),
        cell_grad * old * forget_gate * (1.0 - forget_gate),
        cell_grad * input_gate * (1.0 - cand_gate * cand_gate),
        down * new_tanh * output_gate * (1.0 - output_gate),
    ]
    return output_gate * new_tanh, new, cell_grad * forget_gate, jnp.concatenate(grads, 0)


def forward_kernel(
    stacked, from_next, from_pair, kernel, bias, cell_prev, grad_hidden, grad_cell,
    hidden, cell, grad_cell_prev, grads, terms, weights,
    hidden_rows, hidden_here, cell_here, back_here, sems,
):
    depth = kernel.shape[0] // 3
    blank = jnp.zeros((STACK - depth, kernel.shape[1]), F32)
    for row_off in range(3):
        part = kernel[...].astype(F32)[row_off * depth : (row_off + 1) * depth]
        weights[:, row_off * STACK : (row_off + 1) * STACK] = jnp.concatenate([part, blank], 0).T.astype(BF16)
    units = bias.shape[0] // 4
    height = cell_prev.shape[0] // units
    channels = (from_pair.shape[0] - 3 * units) // 2
    top, bottom = in_order(from_next, from_pair, NS[-1])
    north = [stack_of(top[i * channels : (i + 1) * channels]) for i in range(2)]
    south = [stack_of(bottom[i * channels : (i + 1) * channels]) for i in range(2)]

    def two_rows(place):
        if 2 <= place <= height:
            return stacked[:, (place - 2) * LANES : place * LANES]
        outer = [None] * (height + 4)
        outer[:2], outer[-2:] = north, south
        outer[2], outer[-3] = stacked[:, :LANES], stacked[:, (height - 1) * LANES :]
        return jnp.concatenate(outer[place : place + 2], 1)

    def copy_out(half):
        rows = pl.ds(half * (height // 2), height // 2)
        return [
            pltpu.make_async_copy(here.at[:, rows, :], out.at[:, rows, :], sems.at[2 * half + i])
            for i, (here, out) in enumerate(((cell_here, cell), (back_here, grad_cell_prev)))
        ]

    cell_rows = cell_here.reshape(units * height, LANES)
    back_rows = back_here.reshape(units * height, LANES)
    bias_cells = jnp.broadcast_to(bias[...], (4 * units, LANES))
    lane = lax.broadcasted_iota(jnp.int32, (4 * units, LANES), 1)
    middle = (lane > 0) & (lane < LANES - 1)
    for pair in range(height // 2 + 1):
        sums = jnp.zeros((4 * units, 2 * LANES), F32)
        for row_off in range(3):
            sums = sums + jnp.dot(
                weights[:, row_off * STACK : (row_off + 1) * STACK],
                two_rows(2 * pair + row_off),
                preferred_element_type=F32,
            )
        for half in range(2):
            place = 2 * pair + half
            gates = sums[:, half * LANES : (half + 1) * LANES] + bias_cells
            inside = 0 < place <= height
            if inside:
                at = pl.ds(place - 1, units, stride=height)
                states = [cell_prev[at, :], grad_hidden[at, :], grad_cell[at, :]]
            else:
                rows = bottom if place else top
                states = [rows[2 * channels + i * units : 2 * channels + (i + 1) * units] for i in range(3)]
            new_hidden, new, down, row_grads = gate_step(gates, *states)
            grads[:, place * LANES : (place + 1) * LANES] = jnp.where(middle, row_grads, 0.0).astype(BF16)
            if inside:
                hidden_rows[at, :] = new_hidden
                cell_rows[at, :] = new
                back_rows[at, :] = down
        if pair == height // 4:
            for copy in copy_out(0):
                copy.start()
    hidden_here[...] = hidden_rows[...].astype(BF16)
    hidden_copy = pltpu.make_async_copy(hidden_here, hidden, sems.at[4])
    copies = copy_out(0) + copy_out(1) + [hidden_copy]
    for copy in copies[2:]:
        copy.start()
    own = grads[:, LANES : (height + 1) * LANES]
    for row_off in range(3):
        if row_off == 0:
            rows = jnp.concatenate([north[1], stacked[:, : (height - 1) * LANES]], 1)
        elif row_off == 1:
            rows = stacked[...]
        else:
            rows = jnp.concatenate([stacked[:, LANES:], south[0]], 1)
        terms[row_off * STACK : (row_off + 1) * STACK] = lax.dot_general(
            rows, own, (((1,), (1,)), ((), ())), preferred_element_type=F32
        )
    for copy in copies:
        copy.wait()


def sides_kernel(
    columns, from_next, from_pair, weights, bias, inner_terms, side_grads, side_cells, terms, *, height
):
    units = bias.shape[0] // 4
    channels = columns.shape[0] - units
    spare = STACK - 3 * channels
    west, east = in_order(from_next, from_pair, EW[-1])
    west, east = west[:channels], east[:channels]
    slot = lax.broadcasted_iota(jnp.int32, (channels, LANES), 1) % STEP
    own = columns[:channels]
    outer = jnp.where(slot < 2, west, moved(east, 2))
    before = by_slot(slot, outer, moved(own, 1), moved(outer, 1), moved(own, 2))
    at = by_slot(slot, moved(outer, -1), own, own, moved(outer, 1))
    after = by_slot(slot, moved(own, -2), moved(outer, -1), moved(own, -1), outer)
    patches = jnp.concatenate([before, at, after], 0)
    ones_row = (lax.broadcasted_iota(jnp.int32, (spare, LANES), 0) == 0).astype(F32)
    stacks = [
        jnp.concatenate([moved(patches, -STEP * row_off), ones_row], 0).astype(BF16)
        for row_off in range(3)
    ]
    gates = jnp.broadcast_to(bias[...], (4 * units, LANES))
    for row_off in range(3):
        gates = gates + jnp.dot(
            weights[:, row_off * STACK : (row_off + 1) * STACK], stacks[row_off], preferred_element_type=F32
        )
    slot = slot[:units]
    here, west, east = columns[channels:], west[:units], east[:units]
    old = by_slot(slot, moved(west, -2), moved(here, 1), moved(here, 1), moved(east, 1))
    down = by_slot(slot, moved(west, -3), moved(here, -1), moved(here, -1), east)
    grad_cell = by_slot(slot, moved(west, -4), moved(here, -3), moved(here, -3), moved(east, -1))
    new_hidden, new, back, grads = gate_step(gates, old, down, grad_cell)
    side_cells[:units] = new_hidden
    side_cells[units : 2 * units] = new
    side_cells[2 * units :] = back
    side_grads[...] = grads.astype(BF16)
    lane = lax.broadcasted_iota(jnp.int32, grads.shape, 1)
    slot = lane % STEP
    inside = (lane >= STEP) & (lane < STEP * (height + 1)) & ((slot == 1) | (slot == 2))
    grads = jnp.where(inside, grads, 0.0).astype(BF16)
    for row_off in range(3):
        total = inner_terms[row_off * STACK : (row_off + 1) * STACK] + lax.dot_general(
            stacks[row_off], grads, (((1,), (1,)), ((), ())), preferred_element_type=F32
        )
        for half in range(2):
            start = (3 * half + row_off) * STACK
            terms[start : start + STACK] = total[:, half * LANES : (half + 1) * LANES].astype(BF16)


def backward_kernel(
    weights, grads, side_grads, side_cells, inner_hidden, inner_cell, inner_back,
    hidden, cell, grad_cell_prev, grad_frame, grad_hidden_prev,
    sums, rows,
):
    height = grads.shape[1] // LANES - 2
    units = hidden.shape[0] // height
    inputs = grad_frame.shape[0] // height
    channels = inputs + units
    lane = lax.broadcasted_iota(jnp.int32, (channels, LANES), 1)
    ends = (lane[:units] == 0) | (lane[:units] == LANES - 1)
    rows[: units * height] = inner_hidden[...].astype(F32)
    for n in range(height):
        at = pl.ds(n, units, stride=height)
        for i, (inner, out) in enumerate(((rows, rows), (inner_cell, cell), (inner_back, grad_cell_prev))):
            side = pltpu.roll(side_cells[i * units : (i + 1) * units], LANES - STEP * (n + 1) - 2, 1)
            out[at, :] = jnp.where(ends, side, inner[at, :])
    hidden[...] = rows[: units * height].astype(BF16)

    outer = jnp.dot(weights[...], side_grads[...], preferred_element_type=F32)
    parts = []
    for col_off in range(3):
        part = jnp.zeros((channels, LANES), F32)
        for row_off in range(3):
            start = (3 * row_off + col_off) * channels
            piece = outer[start : start + channels]
            part = part + moved(piece, -STEP * (2 - row_off))
        parts.append(part)
    slot = lane % STEP
    sides = jnp.where((slot == 1) | (slot == 2), parts[1], 0.0) + jnp.where(
        slot == 0,
        pltpu.roll(parts[0], LANES - 1, 1),
        jnp.where(
            slot == 1,
            pltpu.roll(parts[0], LANES - 2, 1),
            jnp.where(slot == 2, pltpu.roll(parts[2], 2, 1), pltpu.roll(parts[2], 1, 1)),
        ),
    )
    for place in range(0, height + 2, 2):
        cells = grads[:, place * LANES : (place + 2) * LANES]
        product = jnp.dot(weights[...], cells, preferred_element_type=F32)
        for half in range(2):
            for row_off in range(3):
                n = place + half + row_off - 2
                if not 0 <= n < height:
                    continue
                for col_off in range(3):
                    start = (3 * row_off + col_off) * channels
                    piece = product[start : start + channels, half * LANES : (half + 1) * LANES]
                    if row_off == 2:
                        sums[n, col_off] = piece
                    else:
                        sums[n, col_off] = sums[n, col_off] + piece
    edge = (lane < 2) | (lane >= LANES - 2)
    for n in range(height):
        total = sums[n, 1] + pltpu.roll(sums[n, 0], LANES - 1, 1) + pltpu.roll(sums[n, 2], 1, 1)
        total = total + jnp.where(edge, moved(sides, -STEP * n - 2), 0.0)
        rows[pl.ds(n, channels, stride=height), :] = total
    grad_frame[...] = rows[: inputs * height].astype(BF16)
    grad_hidden_prev[...] = rows[inputs * height :].astype(BF16)


def finish_kernel(total, kernel_step, bias_step):
    block = kernel_step.shape[0] // 3
    halves = [total[half * 3 * STACK : (half + 1) * 3 * STACK].astype(F32) for half in range(2)]
    whole = jnp.concatenate(halves, 1)
    parts = [whole[i * STACK : i * STACK + block] for i in range(3)]
    bias_grad = whole[block : block + 1]
    norm = jnp.sqrt(sum(jnp.sum(part * part) for part in parts) + jnp.sum(bias_grad * bias_grad))
    factor = jnp.minimum(1.0, CLIP_NORM / norm)
    for i, part in enumerate(parts):
        kernel_step[i * block : (i + 1) * block] = part * factor
    bias_step[...] = bias_grad * factor


def sum_kernel(parts, copies):
    total = jnp.sum(parts[...].astype(F32), 0).astype(copies.dtype)
    copies[...] = jnp.broadcast_to(total[None], copies.shape)


def summed(parts, copies, kind):
    return pl.pallas_call(
        sum_kernel,
        out_shape=jax.ShapeDtypeStruct((copies,) + parts.shape[1:], kind),
        in_specs=vmem(1),
        out_specs=vmem(1)[0],
        compiler_params=pltpu.CompilerParams(vmem_limit_bytes=8 * 2**20),
    )(parts)


def exchanged(copies, axes):
    return lax.all_to_all(copies, axes, 0, 0, tiled=True)


def shape(rows, columns, kind):
    return jax.ShapeDtypeStruct((rows, columns), kind)


def called(kernel, outs, scratch, cost, *args, aliases={}):
    return pl.pallas_call(
        kernel,
        out_shape=tuple(outs),
        in_specs=vmem(len(args)),
        out_specs=tuple(vmem(len(outs))),
        scratch_shapes=scratch,
        input_output_aliases=aliases,
        compiler_params=pltpu.CompilerParams(vmem_limit_bytes=16 * 2**20),
        cost_estimate=pl.CostEstimate(flops=cost, bytes_accessed=2 * cost // 1000, transcendentals=0),
    )(*args)


def per_device(frame, hidden_prev, cell_prev, kernel, bias, grad_hidden, grad_cell):
    inputs, height, breadth = frame.shape
    units = hidden_prev.shape[0]
    channels = inputs + units
    gate_rows = kernel.shape[0]
    flat = (units * height, breadth)
    states = (cell_prev.reshape(flat), grad_hidden.reshape(flat), grad_cell.reshape(flat))

    strip = shape(2 * channels + 3 * units, breadth, BF16)
    blocks = (frame.reshape(inputs * height, breadth), hidden_prev.reshape(flat), *states)
    channel_rows = (channels * height, breadth)
    arrays = (frame, hidden_prev, cell_prev, grad_hidden, grad_cell)
    to_pair, to_next = pl.pallas_call(
        rows_kernel,
        out_shape=(strip, strip),
        in_specs=[pl.BlockSpec(memory_space=pl.ANY)] * 5,
        out_specs=tuple(vmem(2)),
        scratch_shapes=[
            pltpu.VMEM(channel_rows, F32),
            pltpu.VMEM(frame.shape, BF16),
            pltpu.VMEM(hidden_prev.shape, BF16),
            pltpu.VMEM((2, 3, units, breadth), F32),
            pltpu.SemaphoreType.DMA((8,)),
        ],
        compiler_params=pltpu.CompilerParams(vmem_limit_bytes=60 * 2**20),
        cost_estimate=pl.CostEstimate(flops=1_000_000, bytes_accessed=1_000_000, transcendentals=0),
    )(*arrays)
    edge = shape(channels + units, LANES, F32)
    columns, stacked = called(
        functools.partial(columns_kernel, height=height),
        [edge, shape(STACK, height * breadth, BF16)],
        [pltpu.VMEM(channel_rows, F32)],
        1_000_000,
        *blocks,
    )
    rows = swapped(to_pair, to_next, NS)
    sent = shape(-(-channels // 16) * 16, LANES, BF16)
    columns, to_next, to_pair = called(
        functools.partial(corners_kernel, height=height, units=units), [edge, sent, sent], [], 100_000, columns, *rows
    )
    sides = swapped(to_pair, to_next, EW)
    bias = bias[:, None]
    field = shape(*flat, F32)
    cube = jax.ShapeDtypeStruct((units, height, breadth), F32)
    inner_hidden, inner_cell, inner_back, grads, inner_terms, weights = pl.pallas_call(
        forward_kernel,
        out_shape=(
            shape(*flat, BF16),
            cube,
            cube,
            shape(gate_rows, (height + 2) * breadth, BF16),
            shape(3 * STACK, gate_rows, F32),
            shape(gate_rows, 3 * STACK, BF16),
        ),
        in_specs=vmem(8),
        out_specs=tuple([pl.BlockSpec(memory_space=pl.ANY)] * 3 + vmem(3)),
        scratch_shapes=[
            pltpu.VMEM(flat, F32),
            pltpu.VMEM(flat, BF16),
            pltpu.VMEM(cube.shape, F32),
            pltpu.VMEM(cube.shape, F32),
            pltpu.SemaphoreType.DMA((5,)),
        ],
        compiler_params=pltpu.CompilerParams(vmem_limit_bytes=16 * 2**20),
        cost_estimate=pl.CostEstimate(flops=1_400_000_000, bytes_accessed=4_000_000, transcendentals=700_000),
    )(stacked, *rows, kernel.T, bias, *states)
    side_grads, side_cells, terms = called(
        functools.partial(sides_kernel, height=height),
        [shape(gate_rows, LANES, BF16), shape(3 * units, LANES, F32), shape(6 * STACK, LANES, BF16)],
        [],
        100_000_000,
        columns,
        *sides,
        weights,
        bias,
        inner_terms,
    )

    plane = lax.axis_size(PLANE)
    low, high = lax.axis_size("z_lo"), lax.axis_size("z_hi")
    mine = exchanged(terms.reshape(plane, -1, LANES), PLANE)
    mine = exchanged(summed(mine, low, F32), "z_lo")
    mine = exchanged(summed(mine, high, F32), "z_hi")
    mine = summed(mine, plane, BF16)
    total = exchanged(mine, PLANE).reshape(6 * STACK, LANES)
    hidden, cell, grad_cell_prev, grad_frame, grad_hidden_prev = called(
        backward_kernel,
        [shape(*flat, BF16), field, field, shape(inputs * height, breadth, BF16), shape(*flat, BF16)],
        [pltpu.VMEM((height, 3, channels, breadth), F32), pltpu.VMEM((channels * height, breadth), F32)],
        764_000_000,
        kernel.T,
        grads,
        side_grads,
        side_cells,
        inner_hidden,
        inner_cell.reshape(flat),
        inner_back.reshape(flat),
        aliases={4: 0, 5: 1, 6: 2},
    )
    kernel_step, bias_step = called(
        finish_kernel, [shape(9 * channels, gate_rows, F32), shape(1, gate_rows, F32)], [], 1_000_000, total
    )
    whole = (units, height, breadth)
    return (
        hidden.reshape(whole),
        cell.reshape(whole),
        grad_frame.reshape(frame.shape),
        grad_hidden_prev.reshape(whole),
        grad_cell_prev.reshape(whole),
        kernel_step.T,
        bias_step.reshape(gate_rows),
    )


def solution(mesh):
    mesh = Mesh(mesh.devices.reshape(4, 4, 2, 4, 2, 2), EW + NS)
    grid = P(None, NS, EW)
    return jax.shard_map(
        per_device,
        mesh=mesh,
        in_specs=(grid, grid, grid, P(), P(), grid, grid),
        out_specs=(grid, grid, grid, grid, grid, P(), P()),
        check_vma=False,
    )
```
